32 devices in a mesh: role: 2 (over x), tp: 16 (over z, y, core).
Axes of the slice: x: 2, y: 2, z: 4, core: 2. Of those that a mesh axis runs over, the one named last changes fastest.
Arguments:
- latents: bfloat16 [1024, 3072], P('role'), may hold values from -6 to 6
- fresh_noise: bfloat16 [1024, 3072], P('role', 'tp'), may hold values from -6 to 6
- sigmas: float32 [2], replicated, may hold values from 0.3 to 0.9
- student_up: bfloat16 [3072, 12288], P(None, 'tp'), may hold values from -0.109375 to 0.109375
- student_down: bfloat16 [12288, 3072], P('tp'), may hold values from -0.0546875 to 0.0546875
- score_up: bfloat16 [2, 3072, 12288], P('role', None, 'tp'), may hold values from -0.109375 to 0.109375
- score_down: bfloat16 [2, 12288, 3072], P('role', 'tp'), may hold values from -0.0546875 to 0.0546875
Outputs:
- generated: bfloat16 [1024, 3072], P('role', 'tp')
- grad_up: float32 [3072, 12288], P(None, 'tp')
- grad_down: float32 [12288, 3072], P('tp')
The draws below stay inside these ranges and needn't reach their ends.
All inputs are finite; a program needn't handle non-finite values.
Results may differ from the reference program's by a relative error of at most 0.012.
Values may be sent and summed in bfloat16 or wider, within the bound.
No kernel may reach another device: no remote copies, remote signals or barrier semaphores. Data moves between devices by JAX's collectives and lax.ppermute only.
A program may use at most 192 MiB of HBM per device.

```python
import jax
import jax.numpy as jnp
from jax import lax

D = 3072
FF = 12288
TOKENS = 512
MODELS = 2
IMAGES = 2
ALL_TOK = 1024


def level_of(key, extent, split, least, high):
    def one(axis_at, shards_of):
        steps = jax.random.uniform(jax.random.fold_in(jax.random.fold_in(key, 6), axis_at), (shards_of,), jnp.float32, least / len(split), high / len(split))
        return jnp.repeat(jnp.exp(steps), extent[axis_at] // shards_of).reshape((-1,) + (1,) * (len(extent) - axis_at - 1))

    factor_of = one(*split[0])
    for cut in split[1:]:
        factor_of = factor_of * one(*cut)
    return factor_of


def centred(stream_key, extent, deviation, bound, cuts=(), held_as=jnp.bfloat16):
    gain = level_of(stream_key, extent, cuts, -0.22, 0.18) if cuts else 1.0
    array = jax.random.normal(stream_key, extent, jnp.float32) * deviation * gain
    return jnp.minimum(jnp.maximum(array, -bound), bound).astype(held_as)


def setup_inputs(seed: int = 0) -> dict:
    key_of = jax.random.split(jax.random.key(seed), 8)
    latents = centred(key_of[0], (ALL_TOK, D), 1.0, 6.0, ((0, 2),))
    fresh_noise = centred(key_of[1], (ALL_TOK, D), 1.0, 6.0, ((0, 2), (1, 16)))
    sigmas = jnp.clip(jax.random.uniform(key_of[2], (IMAGES,), jnp.float32, 0.3, 0.9), 0.3, 0.9)
    student_up = centred(key_of[3], (D, FF), D ** -0.5, 0.109375, ((1, 16),))
    student_down = centred(key_of[4], (FF, D), FF ** -0.5, 0.0546875, ((0, 16),))
    score_up = centred(key_of[5], (MODELS, D, FF), D ** -0.5, 0.109375, ((0, 2), (2, 16)))
    score_down = centred(key_of[6], (MODELS, FF, D), FF ** -0.5, 0.0546875, ((0, 2), (1, 16)))
    return dict(latents=latents, fresh_noise=fresh_noise, sigmas=sigmas, student_up=student_up, student_down=student_down, score_up=score_up, score_down=score_down)


def normalize(values):
    floats = values.astype(jnp.float32)
    return floats * lax.rsqrt(lax.optimization_barrier(jnp.mean(floats * floats, axis=-1, keepdims=True)) + 1e-06)

def smooth_gelu(values):
    return jax.nn.gelu(values, approximate=True)

def reference(latents, fresh_noise, sigmas, student_up, student_down, score_up, score_down):
    normed = normalize(latents).astype(jnp.bfloat16)
    preact = jnp.dot(normed, student_up, preferred_element_type=jnp.float32)
    hidden = smooth_gelu(preact).astype(jnp.bfloat16)
    generated = jnp.dot(hidden, student_down, preferred_element_type=jnp.float32).astype(jnp.bfloat16)
    levels = jnp.repeat(sigmas.astype(jnp.float32), TOKENS)[:, None]
    blended = (1.0 - levels) * generated.astype(jnp.float32) + levels * fresh_noise.astype(jnp.float32)
    noised = normalize(blended).astype(jnp.bfloat16)
    velocity = []
    for member in range(MODELS):
        activity = smooth_gelu(jnp.dot(noised, score_up[member], preferred_element_type=jnp.float32)).astype(jnp.bfloat16)
        velocity.append(jnp.dot(activity, score_down[member], preferred_element_type=jnp.float32))
    update = (levels * (velocity[0] - velocity[1])).astype(jnp.bfloat16)
    grad_down = jnp.dot(hidden.T, update, preferred_element_type=jnp.float32)
    backflow = jnp.dot(update, student_down.T, preferred_element_type=jnp.float32)
    _, pullback = jax.vjp(smooth_gelu, preact)
    preact_grad = pullback(backflow)[0].astype(jnp.bfloat16)
    grad_up = jnp.dot(normed.T, preact_grad, preferred_element_type=jnp.float32)
    return (generated, grad_up, grad_down)
```

```python
import jax
import jax.numpy as jnp
from jax import lax
from jax.sharding import PartitionSpec as P

CHUNKS = 1
AXES = ("role", "tp")
BF16 = jnp.bfloat16
F32 = jnp.float32


def normalize(values):
    floats = values.astype(F32)
    return floats * lax.rsqrt(jnp.mean(floats * floats, axis=-1, keepdims=True) + 1e-06)


def smooth_gelu(values):
    return jax.nn.gelu(values, approximate=True)


def dot(a, b, dims):
    return lax.dot_general(a, b, ((dims[:1], dims[1:]), ((), ())), preferred_element_type=F32)


def add(*terms):
    total = terms[0].astype(F32)
    for term in terms[1:]:
        total = total + term.astype(F32)
    return total


def take(array, index, axis):
    return lax.dynamic_index_in_dim(array, index, axis, keepdims=False)


def make_body(roles, shards):
    devices = roles * shards
    depth = shards // 4
    ROLE, PAIR, CORE = shards, 2, 1

    def swap(value, mask):
        return lax.ppermute(value, AXES, [(i, i ^ mask) for i in range(devices)])

    def body(latents, fresh_noise, sigmas, student_up, student_down, score_up, score_down):
        image_rows, width = latents.shape
        block = width // shards
        role = lax.axis_index("role")
        place = lax.axis_index("tp")
        outer, pair, core = place // 4, (place // 2) % 2, place % 2
        score_up, score_down = score_up[0], score_down[0]
        tokens = image_rows // CHUNKS
        own_level = take(sigmas, role, 0)
        other_level = take(sigmas, 1 - role, 0)
        polarity = 1.0 - 2.0 * role.astype(F32)

        def outer_sum(part, axis):
            return add(
                take(part, outer, 0),
                *[swap(take(part, outer ^ k, 0), 4 * k) for k in range(1, depth)],
            )

        def core_sum(term):
            grid = term.reshape(depth, 2, 2, block, term.shape[-1])
            arrived = swap(take(grid, 1 - core, 2), CORE)
            return add(take(grid, core, 2), arrived).astype(BF16)

        def student_sum(term):
            grid = core_sum(term)
            cut = block // 3 // 16 * 16
            first = grid[:, :, :cut]
            later = grid[:, :, cut:]
            kept = add(take(later, pair, 1), swap(take(later, 1 - pair, 1), PAIR)).astype(BF16)
            later = outer_sum(kept, 0)
            if not cut:
                return later
            kept = outer_sum(first, 0).astype(BF16)
            first = add(take(kept, pair, 0), swap(take(kept, 1 - pair, 0), PAIR))
            return jnp.concatenate([first, later], axis=0)

        def gather(part):
            stack = jnp.zeros((depth,) + part.shape, BF16)
            for k in range(depth):
                piece = part if k == 0 else swap(part, 4 * k)
                stack = lax.dynamic_update_index_in_dim(stack, piece, outer ^ k, 0)
            half = block // 2
            by_role = swap(stack, ROLE)
            by_pair = swap(stack, PAIR)
            by_both = jnp.concatenate(
                [swap(by_role[:, :half], PAIR), swap(by_pair[:, half:], ROLE)], axis=1
            )
            images = []
            for near, far in ((stack, by_pair), (by_role, by_both)):
                image = jnp.zeros((depth, 2, 2) + part.shape, BF16)
                for value, row in ((near, pair), (far, 1 - pair)):
                    for held, column in ((value, core), (swap(value, CORE), 1 - core)):
                        image = lax.dynamic_update_slice(
                            image, held[:, None, None], (0, row, column, 0, 0)
                        )
                images.append(image.reshape(width, part.shape[-1]))
            return images

        def scatter(own, other):
            half = block // 2
            other = core_sum(other)
            own = core_sum(own)
            both = take(other, 1 - pair, 1)
            by_role = take(other, pair, 1)
            by_pair = take(own, 1 - pair, 1)
            kept = take(own, pair, 1)
            from_pair = swap(both[:, :half], PAIR)
            from_role = swap(both[:, half:], ROLE)
            by_role = jnp.concatenate(
                [add(by_role[:, :half], from_pair).astype(BF16), by_role[:, half:]], axis=1
            )
            by_pair = jnp.concatenate(
                [by_pair[:, :half], add(by_pair[:, half:], from_role).astype(BF16)], axis=1
            )
            kept = add(kept, swap(by_role, ROLE), swap(by_pair, PAIR)).astype(BF16)
            return outer_sum(kept, 0)

        normed = normalize(latents).astype(BF16)
        share = image_rows // 2
        mine = lax.dynamic_slice_in_dim(normed, core * share, share, 0)
        near = swap(mine, ROLE)
        far = swap(near, CORE)
        normed_other = jnp.zeros((2, share, width), BF16)
        normed_other = lax.dynamic_update_index_in_dim(normed_other, near, core, 0)
        normed_other = lax.dynamic_update_index_in_dim(normed_other, far, 1 - core, 0)
        normed_other = normed_other.reshape(image_rows, width)

        generated, updates, hiddens, preacts = [], [], [], []
        for chunk in range(CHUNKS):
            rows = slice(chunk * tokens, (chunk + 1) * tokens)
            preact = dot(student_up, normed[rows], (0, 1))
            hidden = smooth_gelu(preact).astype(BF16)
            partial = dot(student_down, hidden, (0, 0)).astype(BF16)
            made = student_sum(partial).astype(BF16)
            generated.append(made.T)
            noise = fresh_noise[rows].T.astype(F32)
            blended = (1.0 - own_level) * made.astype(F32) + own_level * noise
            images = gather(blended.astype(BF16))
            terms = []
            for image, level in zip(images, (own_level, other_level)):
                floats = image.astype(F32)
                scale = lax.rsqrt(jnp.mean(floats * floats, axis=0, keepdims=True) + 1e-06)
                activity = smooth_gelu(dot(score_up, image, (0, 0)) * scale).astype(BF16)
                terms.append((polarity * level * dot(score_down, activity, (0, 0))).astype(BF16))
            update = scatter(*terms).astype(BF16)
            updates.append(gather(update))
            preact_other = dot(student_up, normed_other[rows], (0, 1))
            hiddens.append([hidden, smooth_gelu(preact_other).astype(BF16)])
            preacts.append([preact, preact_other])

        grad_up, grad_down = 0.0, 0.0
        for chunk in range(CHUNKS):
            rows = slice(chunk * tokens, (chunk + 1) * tokens)
            update = jnp.concatenate(updates[chunk], axis=1)
            hidden = jnp.concatenate(hiddens[chunk], axis=1)
            preact = jnp.concatenate(preacts[chunk], axis=1)
            inputs = jnp.concatenate([normed[rows], normed_other[rows]], axis=0)
            grad_down = grad_down + dot(hidden, update, (1, 1))
            backflow = dot(student_down, update, (1, 0))
            _, pullback = jax.vjp(smooth_gelu, preact)
            preact_grad = pullback(backflow)[0].astype(BF16)
            grad_up = grad_up + dot(inputs, preact_grad, (0, 1))
        return (jnp.concatenate(generated, axis=0), grad_up, grad_down)

    return body


def solution(mesh):
    return jax.shard_map(
        make_body(mesh.shape["role"], mesh.shape["tp"]),
        mesh=mesh,
        in_specs=(
            P("role", None),
            P("role", "tp"),
            P(),
            P(None, "tp"),
            P("tp", None),
            P("role", None, "tp"),
            P("role", "tp", None),
        ),
        out_specs=(P("role", "tp"), P(None, "tp"), P("tp", None)),
        check_vma=False,
    )
```

```python
import jax
import jax.numpy as jnp
from jax import lax
from jax.experimental import pallas as pl
from jax.experimental.pallas import tpu as pltpu
from jax.sharding import PartitionSpec as P

AXES = ("role", "tp")
BF16 = jnp.bfloat16
F32 = jnp.float32
PARTS = 4
SMEM = pl.BlockSpec(memory_space=pltpu.SMEM)
HBM = pl.BlockSpec(memory_space=pl.ANY)
PARAMS = pltpu.CompilerParams(vmem_limit_bytes=60 * 2**20)


def smooth_gelu(values):
    return jax.nn.gelu(values, approximate=True)


def gelu_slope(x):
    root, cubic = 0.7978845608028654, 0.044715
    bent = jnp.tanh(root * (x + cubic * x * x * x))
    return 0.5 * (1.0 + bent) + 0.5 * x * (1.0 - bent * bent) * root * (1.0 + 3.0 * cubic * x * x)


def dot(a, b, dims):
    return lax.dot_general(a, b, ((dims[:1], dims[1:]), ((), ())), preferred_element_type=F32)


def add(*terms):
    total = terms[0].astype(F32)
    for term in terms[1:]:
        total = total + term.astype(F32)
    return total


def take(array, index, axis):
    return lax.dynamic_index_in_dim(array, index, axis, keepdims=False)


class Copies:
    def __init__(self, sems):
        self.sems, self.used = sems, 0

    def start(self, source, target):
        copy = pltpu.make_async_copy(source, target, self.sems.at[self.used])
        self.used += 1
        copy.start()
        return copy


def wait(copies):
    for copy in copies:
        copy.wait()


def fetch_pieces(copies, place, pieces, layout, image, part, block):
    if not layout:
        height = image.shape[0] // PARTS
        at = pl.ds(part * height, height)
        return [copies.start(pieces[0].at[at], image.at[at])]
    core, pair = place[0], place[1]
    some = pieces[0].shape[0] // PARTS
    started = []
    for outer in range(part * some, (part + 1) * some):
        for piece, (row, column, first) in zip(pieces, layout):
            row = 1 - pair if row else pair
            column = 1 - core if column else core
            at = pl.multiple_of(((outer * 2 + row) * 2 + column) * block + first, 16)
            started.append(copies.start(piece.at[outer], image.at[pl.ds(at, piece.shape[1])]))
    return started


def fetch_tokens(copies, place, halves, tokens):
    if len(halves) == 1:
        return [copies.start(halves[0], tokens)]
    share = halves[0].shape[0]
    return [
        copies.start(half, tokens.at[pl.ds(pl.multiple_of(at * share, 16), share)])
        for half, at in zip(halves, (place[0], 1 - place[0]))
    ]


def split_by_core(copies, place, block, values, whole, out, held, part):
    height = whole.shape[0]
    if len(out) == 1:
        held[part] = values.astype(BF16)
        return [copies.start(held.at[part], out[0].at[pl.ds(part * height, height)])]
    core = place[0]
    whole[...] = values.astype(BF16)
    pairs = height // (2 * block)
    first = part * pairs
    for p in range(pairs):
        for slot, column in enumerate((1 - core, core)):
            at = pl.multiple_of((2 * p + column) * block, 16)
            held[slot, first + p] = whole[pl.ds(at, block)]
    some = pl.ds(first, pairs)
    return [copies.start(held.at[slot, some], target.at[some]) for slot, target in enumerate(out)]


def sum_shapes(shards, width, rows):
    block = width // shards
    if block % 16:
        whole = jax.ShapeDtypeStruct((width, rows), BF16)
        return [whole], pltpu.VMEM((PARTS, width // PARTS, rows), BF16)
    piece = jax.ShapeDtypeStruct((shards // 2, block, rows), BF16)
    return [piece, piece], pltpu.VMEM((2,) + piece.shape, BF16)


def student(place, latents, up, down, shards):
    rows = sum(half.shape[0] for half in latents)
    width, inner = up.shape
    block = width // shards
    part = width // PARTS
    halves = len(latents)
    sums, held = sum_shapes(shards, width, rows)
    count = len(sums)

    def kernel(*refs):
        place, latents, up = refs[0], refs[1 : 1 + halves], refs[1 + halves]
        refs = refs[halves - 1 :]
        if down is None:
            preact, hidden, scale, latents_v, up_v, acc, sems = refs[3:]
        else:
            down_hbm, preact, hidden, scale = refs[3:7]
            out = refs[7 : 7 + count]
            latents_v, up_v, acc, down_v, whole, held, sems = refs[7 + count :]
        copies = Copies(sems)
        loads = []
        for k in range(PARTS):
            at = slice(k * part, (k + 1) * part)
            loads.append(fetch_tokens(copies, place, [half.at[:, at] for half in latents], latents_v.at[:, at]))
            loads[k].append(copies.start(up.at[at], up_v.at[at]))
        if down is not None:
            later = [copies.start(down_hbm.at[:, pl.ds(k * part, part)], down_v.at[:, pl.ds(k * part, part)]) for k in range(PARTS)]
        squares = 0.0
        for k in range(PARTS):
            at = slice(k * part, (k + 1) * part)
            wait(loads[k])
            value = dot(up_v[at], latents_v[:, at], (0, 1))
            acc[...] = value if k == 0 else acc[...] + value
            floats = latents_v[:, at].astype(F32)
            squares = squares + jnp.sum(floats * floats, axis=1, keepdims=True)
        squares = jnp.broadcast_to(squares, (rows, 128)).T[:1]
        factor = lax.rsqrt(squares / width + 1e-06)
        scale[...] = factor
        values = acc[...] * factor
        preact[...] = values
        hidden[...] = smooth_gelu(values).astype(BF16)
        if down is not None:
            stores = []
            for k in range(PARTS):
                later[k].wait()
                value = dot(down_v[:, k * part : (k + 1) * part], hidden[...], (0, 0))
                stores += split_by_core(copies, place, block, value, whole, out, held, k)
            wait(stores)

    scratch = [
        pltpu.VMEM((rows, width), BF16),
        pltpu.VMEM((width, inner), BF16),
        pltpu.VMEM((inner, rows), F32),
    ]
    if down is not None:
        scratch += [pltpu.VMEM((inner, width), BF16), pltpu.VMEM((part, rows), BF16), held]
    out_shape = [
        jax.ShapeDtypeStruct((inner, rows), F32),
        jax.ShapeDtypeStruct((inner, rows), BF16),
        jax.ShapeDtypeStruct((1, rows), F32),
    ]
    vmem = pl.BlockSpec(memory_space=pltpu.VMEM)
    return pl.pallas_call(
        kernel,
        in_specs=[SMEM] + [HBM] * (halves + (1 if down is None else 2)),
        out_specs=[vmem] * 3 + ([] if down is None else [HBM] * count),
        out_shape=out_shape + ([] if down is None else sums),
        scratch_shapes=scratch + [pltpu.SemaphoreType.DMA((6 * PARTS,))],
        compiler_params=PARAMS,
        cost_estimate=pl.CostEstimate(flops=4 * rows * width * inner, bytes_accessed=6 * width * inner, transcendentals=rows * inner),
        name="student_forward",
    )(place, *latents, up, *([] if down is None else [down]))


def score(place, factor, pieces, layout, up, down, shards):
    width, inner = up.shape
    rows = pieces[0].shape[-1]
    block = width // shards
    part = width // PARTS
    count = len(pieces)
    sums, held = sum_shapes(shards, width, rows)

    def kernel(place, factor, *refs):
        pieces, refs = refs[:count], refs[count:]
        up, down = refs[:2]
        out = refs[2 : 2 + len(sums)]
        image, up_v, down_v, acc, active, whole, held, sems = refs[2 + len(sums) :]
        copies = Copies(sems)
        loads = []
        for k in range(PARTS):
            at = slice(k * part, (k + 1) * part)
            loads.append(fetch_pieces(copies, place, pieces, layout, image, k, block) + [copies.start(up.at[at], up_v.at[at])])
        later = [copies.start(down.at[:, pl.ds(k * part, part)], down_v.at[:, pl.ds(k * part, part)]) for k in range(PARTS)]
        squares = 0.0
        for k in range(PARTS):
            at = slice(k * part, (k + 1) * part)
            wait(loads[k])
            value = dot(up_v[at], image[at], (0, 0))
            acc[...] = value if k == 0 else acc[...] + value
            floats = image[at].astype(F32)
            squares = squares + jnp.sum(floats * floats, axis=0, keepdims=True)
        scale = lax.rsqrt(squares / width + 1e-06)
        active[...] = smooth_gelu(acc[...] * scale).astype(BF16)
        stores = []
        for k in range(PARTS):
            later[k].wait()
            value = factor[0] * dot(down_v[:, k * part : (k + 1) * part], active[...], (0, 0))
            stores += split_by_core(copies, place, block, value, whole, out, held, k)
        wait(stores)

    return pl.pallas_call(
        kernel,
        in_specs=[SMEM, SMEM] + [HBM] * (count + 2),
        out_specs=[HBM] * len(sums),
        out_shape=sums,
        scratch_shapes=[
            pltpu.VMEM((width, rows), BF16),
            pltpu.VMEM((width, inner), BF16),
            pltpu.VMEM((inner, width), BF16),
            pltpu.VMEM((inner, rows), F32),
            pltpu.VMEM((inner, rows), BF16),
            pltpu.VMEM((part, rows), BF16),
            held,
            pltpu.SemaphoreType.DMA((4 * PARTS + 2 * shards,)),
        ],
        compiler_params=PARAMS,
        cost_estimate=pl.CostEstimate(flops=4 * rows * width * inner, bytes_accessed=6 * width * inner, transcendentals=rows * inner),
        name="score_member",
    )(place, factor, *pieces, up, down)


def inward_gradient(place, pieces, layout, down, slope, shards):
    inner, width = down.shape
    rows = slope.shape[1]
    part = width // PARTS
    count = len(pieces)

    def kernel(place, *refs):
        pieces, refs = refs[:count], refs[count:]
        down, slope, inward, image, down_v, acc = refs[:6]
        copies = Copies(refs[6])
        loads = []
        for k in range(PARTS):
            at = pl.ds(k * part, part)
            loads.append([copies.start(down.at[:, at], down_v.at[:, at])])
            loads[k] += fetch_pieces(copies, place, pieces, layout, image, k, width // shards)
        for k in range(PARTS):
            at = slice(k * part, (k + 1) * part)
            wait(loads[k])
            value = dot(down_v[:, at], image[at], (1, 0))
            acc[...] = value if k == 0 else acc[...] + value
        inward[...] = (acc[...] * slope[...]).astype(BF16)

    vmem = pl.BlockSpec(memory_space=pltpu.VMEM)
    return pl.pallas_call(
        kernel,
        in_specs=[SMEM] + [HBM] * (count + 1) + [vmem],
        out_specs=vmem,
        out_shape=jax.ShapeDtypeStruct((inner, rows), BF16),
        scratch_shapes=[
            pltpu.VMEM((width, rows), BF16),
            pltpu.VMEM((inner, width), BF16),
            pltpu.VMEM((inner, rows), F32),
            pltpu.SemaphoreType.DMA((PARTS + 2 * shards,)),
        ],
        compiler_params=PARAMS,
        cost_estimate=pl.CostEstimate(flops=2 * rows * width * inner, bytes_accessed=6 * width * inner, transcendentals=0),
        name="inward_gradient",
    )(place, *pieces, down, slope)


def weight_gradients(place, updates, layouts, down, slope, hiddens, tokens, inward, shards):
    inner, width = down.shape
    rows = slope.shape[1]
    block = width // shards
    part = width // PARTS
    counts = [len(pieces) for pieces in updates]
    halves = [len(t) for t in tokens]

    def kernel(place, *refs):
        refs = list(refs)

        def next_refs(number):
            taken = refs[:number]
            del refs[:number]
            return taken

        pieces = [next_refs(number) for number in counts]
        tokens = [next_refs(number) for number in halves]
        down, slope, first, second, before, grad_up, grad_down = next_refs(7)
        images, down_v, slope_v, hiddens_v, acc, inward_v, tokens_v, out_up, out_down, sems = refs
        copies = Copies(sems)

        def load(k):
            at = pl.ds(k * part, part)
            started = fetch_pieces(copies, place, pieces[1], layouts[1], images.at[1], k, block)
            return started + [copies.start(down.at[:, at], down_v.at[:, at])]

        loads = [load(0), load(1)]
        late = [copies.start(slope, slope_v), copies.start(before, inward_v.at[0])]
        near = []
        for k in range(PARTS):
            at = slice(k * part, (k + 1) * part)
            wait(loads[k])
            if k + 2 < PARTS:
                loads.append(load(k + 2))
            elif k + 2 == PARTS:
                for i in range(2):
                    near += fetch_tokens(copies, place, tokens[i], tokens_v.at[i])
            value = dot(down_v[:, at], images[1, at], (1, 0))
            acc[...] = value if k == 0 else acc[...] + value
        wait(late)
        inward_v[1] = (acc[...] * slope_v[...]).astype(BF16)
        far = [copies.start(first, hiddens_v.at[0]), copies.start(second, hiddens_v.at[1])]
        for k in range(PARTS):
            far += fetch_pieces(copies, place, pieces[0], layouts[0], images.at[0], k, block)
        wait(near)
        stores = []
        for k in range(PARTS):
            if k >= 2:
                stores[k - 2].wait()
            at = slice(k * part, (k + 1) * part)
            out_up[k % 2] = dot(tokens_v[0, :, at], inward_v[0], (0, 1)) + dot(tokens_v[1, :, at], inward_v[1], (0, 1))
            stores.append(copies.start(out_up.at[k % 2], grad_up.at[pl.ds(k * part, part)]))
        wait(far)
        for k in range(PARTS):
            if k >= 2:
                stores[PARTS + k - 2].wait()
            at = slice(k * part, (k + 1) * part)
            out_down[k % 2] = dot(hiddens_v[0], images[0, at], (1, 1)) + dot(hiddens_v[1], images[1, at], (1, 1))
            stores.append(copies.start(out_down.at[k % 2], grad_down.at[:, pl.ds(k * part, part)]))
        wait(stores[PARTS - 2 : PARTS] + stores[2 * PARTS - 2 :])

    return pl.pallas_call(
        kernel,
        in_specs=[SMEM] + [HBM] * (sum(counts) + sum(halves) + 5),
        out_specs=[HBM] * 2,
        out_shape=[
            jax.ShapeDtypeStruct((width, inner), F32),
            jax.ShapeDtypeStruct((inner, width), F32),
        ],
        scratch_shapes=[
            pltpu.VMEM((2, width, rows), BF16),
            pltpu.VMEM((inner, width), BF16),
            pltpu.VMEM((inner, rows), F32),
            pltpu.VMEM((2, inner, rows), BF16),
            pltpu.VMEM((inner, rows), F32),
            pltpu.VMEM((2, inner, rows), BF16),
            pltpu.VMEM((2, rows, width), BF16),
            pltpu.VMEM((2, part, inner), F32),
            pltpu.VMEM((2, inner, part), F32),
            pltpu.SemaphoreType.DMA((3 * PARTS + 10 + 4 * shards,)),
        ],
        compiler_params=PARAMS,
        cost_estimate=pl.CostEstimate(flops=10 * rows * width * inner, bytes_accessed=16 * width * inner, transcendentals=0),
        name="weight_gradients",
    )(place, *updates[0], *updates[1], *tokens[0], *tokens[1], down, slope, *hiddens, inward)


def make_body(roles, shards):
    devices = roles * shards
    depth = shards // 4
    ROLE, PAIR, CORE = shards, 2, 1
    columns = [[4 * k + low for k in range(depth)] for low in range(4)]

    def swap(value, mask):
        return lax.ppermute(value, AXES, [(i, i ^ mask) for i in range(devices)])

    def body(latents, fresh_noise, sigmas, student_up, student_down, score_up, score_down):
        rows, width = latents.shape
        block = width // shards
        role = lax.axis_index("role")
        index = lax.axis_index("tp")
        outer, pair, core = index // 4, (index // 2) % 2, index % 2
        place = jnp.stack([core, pair]).astype(jnp.int32)
        own_level = take(sigmas, role, 0)
        other_level = take(sigmas, 1 - role, 0)
        polarity = 1.0 - 2.0 * role.astype(F32)

        def outer_sum(part):
            return add(
                take(part, outer, 0),
                *[swap(take(part, outer ^ k, 0), 4 * k) for k in range(1, depth)],
            )

        def student_sum(grid):
            cut = block // 3 // 16 * 16
            first, later = grid[:, :, :cut], grid[:, :, cut:]
            kept = add(take(later, pair, 1), swap(take(later, 1 - pair, 1), PAIR)).astype(BF16)
            later = outer_sum(kept)
            if not cut:
                return later
            kept = outer_sum(first).astype(BF16)
            first = add(take(kept, pair, 0), swap(take(kept, 1 - pair, 0), PAIR))
            return jnp.concatenate([first, later], axis=0)

        def gather(part, during):
            half = block // 2
            stack = lax.all_gather(part, "tp", axis_index_groups=columns, axis=0)
            by_pair = swap(stack, PAIR)
            by_role = swap(stack, ROLE)
            own = assemble((stack, by_pair, swap(stack, CORE), swap(by_pair, CORE)), OWN)
            by_both = [swap(by_role[:, :half], PAIR), swap(by_pair[:, half:], ROLE)]
            meanwhile = during(*own)
            by_both, meanwhile = lax.optimization_barrier((by_both, meanwhile))
            other = (by_role, *by_both, swap(by_role, CORE), *[swap(piece, CORE) for piece in by_both])
            return own, assemble(other, OTHER), meanwhile

        OWN = ((0, 0, 0), (1, 0, 0), (0, 1, 0), (1, 1, 0))
        OTHER = ((0, 0, 0), (1, 0, 0), (1, 0, block // 2), (0, 1, 0), (1, 1, 0), (1, 1, block // 2))

        def assemble(pieces, layout):
            if block % 32 == 0:
                return pieces, layout
            image = jnp.zeros((depth, 2, 2, block, rows), BF16)
            for piece, (row, column, first) in zip(pieces, layout):
                row = 1 - pair if row else pair
                column = 1 - core if column else core
                image = lax.dynamic_update_slice(image, piece[:, None, None], (0, row, column, first, 0))
            return (image.reshape(width, rows),), ()

        def core_sum(out):
            if len(out) == 1:
                grid = out[0].reshape(depth, 2, 2, block, rows)
                out = take(grid, 1 - core, 2), take(grid, core, 2)
            return add(out[1], swap(out[0], CORE)).astype(BF16).reshape(depth, 2, block, rows)

        def scatter(own, other, during):
            cut = block // 3 // 32 * 32
            rest = block - cut
            half = cut + rest // 2

            def planes(own, other, half):
                both, by_role = take(other, 1 - pair, 0), take(other, pair, 0)
                by_pair, kept = take(own, 1 - pair, 0), take(own, pair, 0)
                axis = both.ndim - 2
                low = lambda array: lax.slice_in_dim(array, 0, half, axis=axis)
                high = lambda array: lax.slice_in_dim(array, half, array.shape[axis], axis=axis)
                from_pair = swap(low(both), PAIR)
                from_role = swap(high(both), ROLE)
                by_role = jnp.concatenate([add(low(by_role), from_pair).astype(BF16), high(by_role)], axis=axis)
                by_pair = jnp.concatenate([low(by_pair), add(high(by_pair), from_role).astype(BF16)], axis=axis)
                return add(kept, swap(by_role, ROLE), swap(by_pair, PAIR))

            result = []
            if cut:
                images = jnp.stack([own[:, :, :cut], other[:, :, :cut]], axis=1)
                images = outer_sum(images).astype(BF16)
            kept = planes(own[:, :, cut:].swapaxes(0, 1), other[:, :, cut:].swapaxes(0, 1), rest // 2).astype(BF16)
            if cut:
                kept, images = lax.optimization_barrier((kept, images))
                result.append(planes(images[0], images[1], cut // 2))
            result.append(outer_sum(kept))
            meanwhile = during()
            return jnp.concatenate(result, axis=0), meanwhile

        share = rows // 2
        near = swap(lax.dynamic_slice_in_dim(latents, core * share, share, 0), ROLE)

        preact, hidden, scale, *out = student(place, (latents,), student_up, student_down, shards)
        made = student_sum(core_sum(out)).astype(BF16)
        noise = fresh_noise.T.astype(F32)
        blended = ((1.0 - own_level) * made.astype(F32) + own_level * noise).astype(BF16)
        slope = gelu_slope(preact) * scale
        blended, near, slope = lax.optimization_barrier((blended, near, slope))
        far = swap(near, CORE)

        def scored(pieces, layout, level):
            return score(place, (polarity * level)[None], pieces, layout, score_up[0], score_down[0], shards)

        _, (pieces, layout), out = gather(blended, lambda *own: scored(*own, own_level))
        own_sum = core_sum(out)
        other_sum = core_sum(scored(pieces, layout, other_level))
        tokens_other, own_sum, other_sum = lax.optimization_barrier(((near, far), own_sum, other_sum))

        def other_forward():
            preact_other, hidden_other, scale_other = student(place, tokens_other, student_up, None, shards)
            return hidden_other, gelu_slope(preact_other) * scale_other

        update, (hidden_other, slope_other) = scatter(own_sum, other_sum, other_forward)
        update, hidden_other, slope_other = lax.optimization_barrier((update.astype(BF16), hidden_other, slope_other))
        (pieces, layout), (pieces_other, layout_other), inward = gather(
            update, lambda *own: inward_gradient(place, *own, student_down, slope, shards)
        )
        grad_up, grad_down = weight_gradients(
            place, (pieces, pieces_other), (layout, layout_other), student_down, slope_other,
            (hidden, hidden_other), ((latents,), tokens_other), inward, shards,
        )
        return (made.T, grad_up, grad_down)

    return body


def solution(mesh):
    return jax.shard_map(
        make_body(mesh.shape["role"], mesh.shape["tp"]),
        mesh=mesh,
        in_specs=(
            P("role", None),
            P("role", "tp"),
            P(),
            P(None, "tp"),
            P("tp", None),
            P("role", None, "tp"),
            P("role", "tp", None),
        ),
        out_specs=(P("role", "tp"), P(None, "tp"), P("tp", None)),
        check_vma=False,
    )
```

```python
import jax
import jax.numpy as jnp
from jax import lax
from jax.experimental import pallas as pl
from jax.experimental.pallas import tpu as pltpu
from jax.sharding import PartitionSpec as P

AXES = ("role", "tp")
BF16 = jnp.bfloat16
F32 = jnp.float32
PARTS = 4
SMEM = pl.BlockSpec(memory_space=pltpu.SMEM)
HBM = pl.BlockSpec(memory_space=pl.ANY)
PARAMS = pltpu.CompilerParams(vmem_limit_bytes=60 * 2**20)


def smooth_gelu(values):
    return jax.nn.gelu(values, approximate=True)


def gelu_slope(x):
    root, cubic = 0.7978845608028654, 0.044715
    bent = jnp.tanh(root * (x + cubic * x * x * x))
    return 0.5 * (1.0 + bent) + 0.5 * x * (1.0 - bent * bent) * root * (1.0 + 3.0 * cubic * x * x)


def dot(a, b, dims):
    return lax.dot_general(a, b, ((dims[:1], dims[1:]), ((), ())), preferred_element_type=F32)


def add(*terms):
    total = terms[0].astype(F32)
    for term in terms[1:]:
        total = total + term.astype(F32)
    return total


def take(array, index, axis):
    return lax.dynamic_index_in_dim(array, index, axis, keepdims=False)


class Copies:
    def __init__(self, sems):
        self.sems, self.used = sems, 0

    def start(self, source, target):
        copy = pltpu.make_async_copy(source, target, self.sems.at[self.used])
        self.used += 1
        copy.start()
        return copy


def wait(copies):
    for copy in copies:
        copy.wait()


def fetch_pieces(copies, place, pieces, layout, image, part, block):
    if not layout:
        height = image.shape[0] // PARTS
        at = pl.ds(part * height, height)
        return [copies.start(pieces[0].at[at], image.at[at])]
    core, pair = place[0], place[1]
    some = pieces[0].shape[0] // PARTS
    started = []
    for outer in range(part * some, (part + 1) * some):
        for piece, (row, column, first) in zip(pieces, layout):
            row = 1 - pair if row else pair
            column = 1 - core if column else core
            at = pl.multiple_of(((outer * 2 + row) * 2 + column) * block + first, 16)
            started.append(copies.start(piece.at[outer], image.at[pl.ds(at, piece.shape[1])]))
    return started


def fetch_tokens(copies, place, halves, tokens):
    if len(halves) == 1:
        return [copies.start(halves[0], tokens)]
    share = halves[0].shape[0]
    return [
        copies.start(half, tokens.at[pl.ds(pl.multiple_of(at * share, 16), share)])
        for half, at in zip(halves, (place[0], 1 - place[0]))
    ]


def split_by_core(copies, place, block, values, out, held, part):
    height = held.shape[1]
    if len(out) == 1:
        held[part] = values.astype(BF16)
        return [copies.start(held.at[part], out[0].at[pl.ds(part * height, height)])]
    core = place[0]
    held[part] = values.astype(BF16)
    pairs = height // (2 * block)
    started = []
    for p in range(pairs):
        for target, column in zip(out, (1 - core, core)):
            at = pl.multiple_of((2 * p + column) * block, 16)
            started.append(copies.start(held.at[part, pl.ds(at, block)], target.at[part * pairs + p]))
    return started


def sum_shapes(shards, width, rows):
    block = width // shards
    held = pltpu.VMEM((PARTS, width // PARTS, rows), BF16)
    if block % 16:
        return [jax.ShapeDtypeStruct((width, rows), BF16)], held
    piece = jax.ShapeDtypeStruct((shards // 2, block, rows), BF16)
    return [piece, piece], held


def student(place, latents, up, down, shards):
    rows = sum(half.shape[0] for half in latents)
    width, inner = up.shape
    block = width // shards
    part = width // PARTS
    halves = len(latents)
    sums, held = sum_shapes(shards, width, rows)
    count = len(sums)

    def kernel(*refs):
        place, latents, up = refs[0], refs[1 : 1 + halves], refs[1 + halves]
        refs = refs[halves - 1 :]
        if down is None:
            preact, hidden, scale, latents_v, up_v, acc, hidden_v, sems = refs[3:]
        else:
            down_hbm, preact, hidden, scale = refs[3:7]
            out = refs[7 : 7 + count]
            latents_v, up_v, acc, hidden_v, down_v, held, sems = refs[7 + count :]
        copies = Copies(sems)
        loads = []
        for k in range(PARTS):
            at = slice(k * part, (k + 1) * part)
            loads.append(fetch_tokens(copies, place, [half.at[:, at] for half in latents], latents_v.at[:, at]))
            loads[k].append(copies.start(up.at[at], up_v.at[at]))
        if down is not None:
            later = [copies.start(down_hbm.at[:, pl.ds(k * part, part)], down_v.at[:, pl.ds(k * part, part)]) for k in range(PARTS)]
        squares = 0.0
        for k in range(PARTS):
            at = slice(k * part, (k + 1) * part)
            wait(loads[k])
            value = dot(up_v[at], latents_v[:, at], (0, 1))
            acc[...] = value if k == 0 else acc[...] + value
            floats = latents_v[:, at].astype(F32)
            squares = squares + jnp.sum(floats * floats, axis=1, keepdims=True)
        squares = jnp.broadcast_to(squares, (rows, 128)).T[:1]
        factor = lax.rsqrt(squares / width + 1e-06)
        scale[...] = factor
        values = acc[...] * factor
        acc[...] = values if down is not None else gelu_slope(values) * factor
        kept = [copies.start(acc, preact)]
        hidden_v[...] = smooth_gelu(values).astype(BF16)
        kept.append(copies.start(hidden_v, hidden))
        if down is not None:
            stores = []
            for k in range(PARTS):
                later[k].wait()
                value = dot(down_v[:, k * part : (k + 1) * part], hidden_v[...], (0, 0))
                stores += split_by_core(copies, place, block, value, out, held, k)
            wait(stores)
        wait(kept)

    scratch = [
        pltpu.VMEM((rows, width), BF16),
        pltpu.VMEM((width, inner), BF16),
        pltpu.VMEM((inner, rows), F32),
        pltpu.VMEM((inner, rows), BF16),
    ]
    if down is not None:
        scratch += [pltpu.VMEM((inner, width), BF16), held]
    out_shape = [
        jax.ShapeDtypeStruct((inner, rows), F32),
        jax.ShapeDtypeStruct((inner, rows), BF16),
        jax.ShapeDtypeStruct((1, rows), F32),
    ]
    vmem = pl.BlockSpec(memory_space=pltpu.VMEM)
    return pl.pallas_call(
        kernel,
        in_specs=[SMEM] + [HBM] * (halves + (1 if down is None else 2)),
        out_specs=[HBM, HBM, vmem] + ([] if down is None else [HBM] * count),
        out_shape=out_shape + ([] if down is None else sums),
        scratch_shapes=scratch + [pltpu.SemaphoreType.DMA((6 * PARTS + shards + 2,))],
        compiler_params=PARAMS,
        cost_estimate=pl.CostEstimate(flops=4 * rows * width * inner, bytes_accessed=6 * width * inner, transcendentals=rows * inner),
        name="student_forward",
    )(place, *latents, up, *([] if down is None else [down]))


def score(place, factor, pieces, layout, up, down, shards):
    width, inner = up.shape
    rows = pieces[0].shape[-1]
    block = width // shards
    part = width // PARTS
    count = len(pieces)
    sums, held = sum_shapes(shards, width, rows)

    def kernel(place, factor, *refs):
        pieces, refs = refs[:count], refs[count:]
        up, down = refs[:2]
        out = refs[2 : 2 + len(sums)]
        image, up_v, down_v, acc, active, held, sems = refs[2 + len(sums) :]
        copies = Copies(sems)
        loads = []
        for k in range(PARTS):
            at = slice(k * part, (k + 1) * part)
            loads.append(fetch_pieces(copies, place, pieces, layout, image, k, block) + [copies.start(up.at[at], up_v.at[at])])
        later = [copies.start(down.at[:, pl.ds(k * part, part)], down_v.at[:, pl.ds(k * part, part)]) for k in range(PARTS)]
        squares = 0.0
        for k in range(PARTS):
            at = slice(k * part, (k + 1) * part)
            wait(loads[k])
            value = dot(up_v[at], image[at], (0, 0))
            acc[...] = value if k == 0 else acc[...] + value
            floats = image[at].astype(F32)
            squares = squares + jnp.sum(floats * floats, axis=0, keepdims=True)
        scale = lax.rsqrt(squares / width + 1e-06)
        active[...] = smooth_gelu(acc[...] * scale).astype(BF16)
        stores = []
        for k in range(PARTS):
            later[k].wait()
            value = factor[0] * dot(down_v[:, k * part : (k + 1) * part], active[...], (0, 0))
            stores += split_by_core(copies, place, block, value, out, held, k)
        wait(stores)

    return pl.pallas_call(
        kernel,
        in_specs=[SMEM, SMEM] + [HBM] * (count + 2),
        out_specs=[HBM] * len(sums),
        out_shape=sums,
        scratch_shapes=[
            pltpu.VMEM((width, rows), BF16),
            pltpu.VMEM((width, inner), BF16),
            pltpu.VMEM((inner, width), BF16),
            pltpu.VMEM((inner, rows), F32),
            pltpu.VMEM((inner, rows), BF16),
            held,
            pltpu.SemaphoreType.DMA((4 * PARTS + 3 * shards,)),
        ],
        compiler_params=PARAMS,
        cost_estimate=pl.CostEstimate(flops=4 * rows * width * inner, bytes_accessed=6 * width * inner, transcendentals=rows * inner),
        name="score_member",
    )(place, factor, *pieces, up, down)


def inward_gradient(place, pieces, layout, down, slope, shards):
    inner, width = down.shape
    rows = slope.shape[1]
    part = width // PARTS
    count = len(pieces)

    def kernel(place, *refs):
        pieces, refs = refs[:count], refs[count:]
        down, slope, inward, image, down_v, acc = refs[:6]
        copies = Copies(refs[6])
        loads = []
        for k in range(PARTS):
            at = pl.ds(k * part, part)
            loads.append([copies.start(down.at[:, at], down_v.at[:, at])])
            loads[k] += fetch_pieces(copies, place, pieces, layout, image, k, width // shards)
        for k in range(PARTS):
            at = slice(k * part, (k + 1) * part)
            wait(loads[k])
            value = dot(down_v[:, at], image[at], (1, 0))
            acc[...] = value if k == 0 else acc[...] + value
        inward[...] = (acc[...] * slope[...]).astype(BF16)

    vmem = pl.BlockSpec(memory_space=pltpu.VMEM)
    return pl.pallas_call(
        kernel,
        in_specs=[SMEM] + [HBM] * (count + 1) + [vmem],
        out_specs=vmem,
        out_shape=jax.ShapeDtypeStruct((inner, rows), BF16),
        scratch_shapes=[
            pltpu.VMEM((width, rows), BF16),
            pltpu.VMEM((inner, width), BF16),
            pltpu.VMEM((inner, rows), F32),
            pltpu.SemaphoreType.DMA((PARTS + 2 * shards,)),
        ],
        compiler_params=PARAMS,
        cost_estimate=pl.CostEstimate(flops=2 * rows * width * inner, bytes_accessed=6 * width * inner, transcendentals=0),
        name="inward_gradient",
    )(place, *pieces, down, slope)


def weight_gradients(place, updates, layouts, down, slope, hiddens, tokens, inward, shards):
    inner, width = down.shape
    rows = slope.shape[1]
    block = width // shards
    part = width // PARTS
    counts = [len(pieces) for pieces in updates]
    halves = [len(t) for t in tokens]

    def kernel(place, *refs):
        refs = list(refs)

        def next_refs(number):
            taken = refs[:number]
            del refs[:number]
            return taken

        pieces = [next_refs(number) for number in counts]
        tokens = [next_refs(number) for number in halves]
        down, slope, first, second, before, grad_up, grad_down = next_refs(7)
        images, down_v, slope_v, hiddens_v, acc, inward_v, tokens_v, out_up, out_down, sems = refs
        copies = Copies(sems)

        def load(k):
            at = pl.ds(k * part, part)
            started = fetch_pieces(copies, place, pieces[1], layouts[1], images.at[:, pl.ds(rows, rows)], k, block)
            return started + [copies.start(down.at[:, at], down_v.at[:, at])]

        loads = [load(k) for k in range(PARTS)]
        late = [copies.start(slope, slope_v), copies.start(before, inward_v.at[:, pl.ds(0, rows)])]
        near = []
        for i in range(2):
            near += fetch_tokens(copies, place, tokens[i], tokens_v.at[pl.ds(i * rows, rows)])
        for k in range(PARTS):
            at = slice(k * part, (k + 1) * part)
            wait(loads[k])
            value = dot(down_v[:, at], images[at, rows:], (1, 0))
            acc[...] = value if k == 0 else acc[...] + value
        wait(late)
        inward_v[:, rows:] = (acc[...] * slope_v[...]).astype(BF16)
        far = [copies.start(first, hiddens_v.at[:, pl.ds(0, rows)]), copies.start(second, hiddens_v.at[:, pl.ds(rows, rows)])]
        for k in range(PARTS):
            far += fetch_pieces(copies, place, pieces[0], layouts[0], images.at[:, pl.ds(0, rows)], k, block)
        wait(near)
        stores = []
        for k in range(PARTS):
            at = slice(k * part, (k + 1) * part)
            out_up[k] = dot(tokens_v[:, at], inward_v[...], (0, 1))
            stores.append(copies.start(out_up.at[k], grad_up.at[pl.ds(k * part, part)]))
        wait(far)
        for k in range(PARTS):
            at = slice(k * part, (k + 1) * part)
            out_down[k] = dot(hiddens_v[...], images[at], (1, 1))
            stores.append(copies.start(out_down.at[k], grad_down.at[:, pl.ds(k * part, part)]))
        wait(stores)

    return pl.pallas_call(
        kernel,
        in_specs=[SMEM] + [HBM] * (sum(counts) + sum(halves) + 5),
        out_specs=[HBM] * 2,
        out_shape=[
            jax.ShapeDtypeStruct((width, inner), F32),
            jax.ShapeDtypeStruct((inner, width), F32),
        ],
        scratch_shapes=[
            pltpu.VMEM((width, 2 * rows), BF16),
            pltpu.VMEM((inner, width), BF16),
            pltpu.VMEM((inner, rows), F32),
            pltpu.VMEM((inner, 2 * rows), BF16),
            pltpu.VMEM((inner, rows), F32),
            pltpu.VMEM((inner, 2 * rows), BF16),
            pltpu.VMEM((2 * rows, width), BF16),
            pltpu.VMEM((PARTS, part, inner), F32),
            pltpu.VMEM((PARTS, inner, part), F32),
            pltpu.SemaphoreType.DMA((3 * PARTS + 10 + 4 * shards,)),
        ],
        compiler_params=PARAMS,
        cost_estimate=pl.CostEstimate(flops=10 * rows * width * inner, bytes_accessed=16 * width * inner, transcendentals=0),
        name="weight_gradients",
    )(place, *updates[0], *updates[1], *tokens[0], *tokens[1], down, slope, *hiddens, inward)


def make_body(roles, shards):
    devices = roles * shards
    depth = shards // 4
    ROLE, PAIR, CORE = shards, 2, 1
    columns = [[4 * k + low for k in range(depth)] for low in range(4)]

    def swap(value, mask):
        return lax.ppermute(value, AXES, [(i, i ^ mask) for i in range(devices)])

    def body(latents, fresh_noise, sigmas, student_up, student_down, score_up, score_down):
        rows, width = latents.shape
        block = width // shards
        role = lax.axis_index("role")
        index = lax.axis_index("tp")
        outer, pair, core = index // 4, (index // 2) % 2, index % 2
        place = jnp.stack([core, pair]).astype(jnp.int32)
        own_level = take(sigmas, role, 0)
        other_level = take(sigmas, 1 - role, 0)
        polarity = 1.0 - 2.0 * role.astype(F32)

        def outer_swaps(part, steps):
            return [swap(take(part, outer ^ k, 0), 4 * k) for k in steps]

        def outer_sum(part):
            return add(take(part, outer, 0), *outer_swaps(part, range(1, depth)))

        def student_sum(grid):
            cut = block // 3 // 16 * 16
            first, later = grid[:, :, :cut], grid[:, :, cut:]
            kept = add(take(later, pair, 1), swap(take(later, 1 - pair, 1), PAIR)).astype(BF16)
            later = outer_sum(kept)
            if not cut:
                return later
            kept = outer_sum(first).astype(BF16)
            first = add(take(kept, pair, 0), swap(take(kept, 1 - pair, 0), PAIR))
            return jnp.concatenate([first, later], axis=0)

        def gather(part, during):
            half = block // 2
            stack = lax.all_gather(part, "tp", axis_index_groups=columns, axis=0)
            by_pair = swap(stack, PAIR)
            by_role = swap(stack, ROLE)
            own = assemble((stack, by_pair, swap(stack, CORE), swap(by_pair, CORE)), OWN)
            by_both = [swap(by_role[:, :half], PAIR), swap(by_pair[:, half:], ROLE)]
            meanwhile = during(*own)
            by_both, meanwhile = lax.optimization_barrier((by_both, meanwhile))
            other = (by_role, *by_both, swap(by_role, CORE), *[swap(piece, CORE) for piece in by_both])
            return own, assemble(other, OTHER), meanwhile

        OWN = ((0, 0, 0), (1, 0, 0), (0, 1, 0), (1, 1, 0))
        OTHER = ((0, 0, 0), (1, 0, 0), (1, 0, block // 2), (0, 1, 0), (1, 1, 0), (1, 1, block // 2))

        def assemble(pieces, layout):
            if block % 32 == 0:
                return pieces, layout
            image = jnp.zeros((depth, 2, 2, block, rows), BF16)
            for piece, (row, column, first) in zip(pieces, layout):
                row = 1 - pair if row else pair
                column = 1 - core if column else core
                image = lax.dynamic_update_slice(image, piece[:, None, None], (0, row, column, first, 0))
            return (image.reshape(width, rows),), ()

        def core_sum(out):
            if len(out) == 1:
                grid = out[0].reshape(depth, 2, 2, block, rows)
                out = take(grid, 1 - core, 2), take(grid, core, 2)
            return add(out[1], swap(out[0], CORE)).astype(BF16).reshape(depth, 2, block, rows)

        def scatter(own, other, during):
            cut = block // 3 // 32 * 32
            rest = block - cut
            half = cut + rest // 2

            def planes(own, other, half):
                both, by_role = take(other, 1 - pair, 0), take(other, pair, 0)
                by_pair, kept = take(own, 1 - pair, 0), take(own, pair, 0)
                axis = both.ndim - 2
                low = lambda array: lax.slice_in_dim(array, 0, half, axis=axis)
                high = lambda array: lax.slice_in_dim(array, half, array.shape[axis], axis=axis)
                from_pair = swap(low(both), PAIR)
                from_role = swap(high(both), ROLE)
                by_role = jnp.concatenate([add(low(by_role), from_pair).astype(BF16), high(by_role)], axis=axis)
                by_pair = jnp.concatenate([low(by_pair), add(high(by_pair), from_role).astype(BF16)], axis=axis)
                return add(kept, swap(by_role, ROLE), swap(by_pair, PAIR)).astype(BF16)

            result = []
            if cut:
                images = jnp.stack([own[:, :, :cut], other[:, :, :cut]], axis=1)
                images = outer_sum(images).astype(BF16)
            kept = planes(own[:, :, cut:].swapaxes(0, 1), other[:, :, cut:].swapaxes(0, 1), rest // 2)
            if cut:
                kept, images = lax.optimization_barrier((kept, images))
                result.append(
                    add(
                        take(images[0], pair, 0),
                        swap(take(images[0], 1 - pair, 0), PAIR),
                        swap(take(images[1], pair, 0), ROLE),
                        swap(take(images[1], 1 - pair, 0), ROLE | PAIR),
                    )
                )
            result.append(outer_sum(kept))
            return jnp.concatenate(result, axis=0), during()

        share = rows // 2
        near = swap(lax.dynamic_slice_in_dim(latents, core * share, share, 0), ROLE)

        preact, hidden, scale, *out = student(place, (latents,), student_up, student_down, shards)
        made = student_sum(core_sum(out)).astype(BF16)
        noise = fresh_noise.T.astype(F32)
        blended = ((1.0 - own_level) * made.astype(F32) + own_level * noise).astype(BF16)
        slope = gelu_slope(preact) * scale
        blended, near, slope = lax.optimization_barrier((blended, near, slope))
        far = swap(near, CORE)

        def scored(pieces, layout, level):
            return score(place, (polarity * level)[None], pieces, layout, score_up[0], score_down[0], shards)

        _, (pieces, layout), out = gather(blended, lambda *own: scored(*own, own_level))
        own_sum = core_sum(out)
        other_sum = core_sum(scored(pieces, layout, other_level))

        tokens_other, own_sum, other_sum = lax.optimization_barrier(((near, far), own_sum, other_sum))

        def other_forward():
            slope_other, hidden_other, _ = student(place, tokens_other, student_up, None, shards)
            return hidden_other, slope_other

        update, (hidden_other, slope_other) = scatter(own_sum, other_sum, other_forward)
        update, hidden_other, slope_other = lax.optimization_barrier((update.astype(BF16), hidden_other, slope_other))
        (pieces, layout), (pieces_other, layout_other), inward = gather(
            update, lambda *own: inward_gradient(place, *own, student_down, slope, shards)
        )
        grad_up, grad_down = weight_gradients(
            place, (pieces, pieces_other), (layout, layout_other), student_down, slope_other,
            (hidden, hidden_other), ((latents,), tokens_other), inward, shards,
        )
        return (made.T, grad_up, grad_down)

    return body


def solution(mesh):
    return jax.shard_map(
        make_body(mesh.shape["role"], mesh.shape["tp"]),
        mesh=mesh,
        in_specs=(
            P("role", None),
            P("role", "tp"),
            P(),
            P(None, "tp"),
            P("tp", None),
            P("role", None, "tp"),
            P("role", "tp", None),
        ),
        out_specs=(P("role", "tp"), P(None, "tp"), P("tp", None)),
        check_vma=False,
    )
```

```python
import jax
import jax.numpy as jnp
from jax import lax
from jax.experimental import pallas as pl
from jax.experimental.pallas import tpu as pltpu
from jax.sharding import PartitionSpec as P

AXES = ("role", "tp")
BF16 = jnp.bfloat16
F32 = jnp.float32
PARTS = 4
SMEM = pl.BlockSpec(memory_space=pltpu.SMEM)
HBM = pl.BlockSpec(memory_space=pl.ANY)
PARAMS = pltpu.CompilerParams(vmem_limit_bytes=60 * 2**20)


def smooth_gelu(values):
    return jax.nn.gelu(values, approximate=True)


def gelu_slope(x):
    root, cubic = 0.7978845608028654, 0.044715
    bent = jnp.tanh(root * (x + cubic * x * x * x))
    return 0.5 * (1.0 + bent) + 0.5 * x * (1.0 - bent * bent) * root * (1.0 + 3.0 * cubic * x * x)


def dot(a, b, dims):
    return lax.dot_general(a, b, ((dims[:1], dims[1:]), ((), ())), preferred_element_type=F32)


def add(*terms):
    total = terms[0].astype(F32)
    for term in terms[1:]:
        total = total + term.astype(F32)
    return total


def take(array, index, axis):
    return lax.dynamic_index_in_dim(array, index, axis, keepdims=False)


class Copies:
    def __init__(self, sems):
        self.sems, self.used = sems, 0

    def start(self, source, target):
        copy = pltpu.make_async_copy(source, target, self.sems.at[self.used])
        self.used += 1
        copy.start()
        return copy


def wait(copies):
    for copy in copies:
        copy.wait()


def fetch_pieces(copies, place, pieces, layout, image, part, block):
    if not layout:
        height = image.shape[0] // PARTS
        at = pl.ds(part * height, height)
        return [copies.start(pieces[0].at[at], image.at[at])]
    core, pair = place[0], place[1]
    some = pieces[0].shape[0] // PARTS
    started = []
    for outer in range(part * some, (part + 1) * some):
        for piece, (row, column, first) in zip(pieces, layout):
            row = 1 - pair if row else pair
            column = 1 - core if column else core
            at = pl.multiple_of(((outer * 2 + row) * 2 + column) * block + first, 16)
            started.append(copies.start(piece.at[outer], image.at[pl.ds(at, piece.shape[1])]))
    return started


def fetch_tokens(copies, place, halves, tokens):
    if len(halves) == 1:
        return [copies.start(halves[0], tokens)]
    share = halves[0].shape[0]
    return [
        copies.start(half, tokens.at[pl.ds(pl.multiple_of(at * share, 16), share)])
        for half, at in zip(halves, (place[0], 1 - place[0]))
    ]


def split_by_core(copies, place, block, values, out, held, part):
    height = held.shape[1]
    if len(out) == 1:
        held[part] = values.astype(BF16)
        return [copies.start(held.at[part], out[0].at[pl.ds(part * height, height)])]
    core = place[0]
    held[part] = values.astype(BF16)
    pairs = height // (2 * block)
    started = []
    for p in range(pairs):
        for target, column in zip(out, (1 - core, core)):
            at = pl.multiple_of((2 * p + column) * block, 16)
            started.append(copies.start(held.at[part, pl.ds(at, block)], target.at[part * pairs + p]))
    return started


def sum_shapes(shards, width, rows):
    block = width // shards
    held = pltpu.VMEM((PARTS, width // PARTS, rows), BF16)
    if block % 16:
        return [jax.ShapeDtypeStruct((width, rows), BF16)], held
    piece = jax.ShapeDtypeStruct((shards // 2, block, rows), BF16)
    return [piece, piece], held


def student(place, latents, up, down, shards):
    rows = sum(half.shape[0] for half in latents)
    width, inner = up.shape
    block = width // shards
    part = width // PARTS
    halves = len(latents)
    sums, held = sum_shapes(shards, width, rows)
    count = len(sums)

    def kernel(*refs):
        place, latents, up = refs[0], refs[1 : 1 + halves], refs[1 + halves]
        refs = refs[halves - 1 :]
        if down is None:
            preact, hidden, scale, latents_v, up_v, acc, hidden_v, sems = refs[3:]
        else:
            down_hbm, preact, hidden, scale = refs[3:7]
            out = refs[7 : 7 + count]
            latents_v, up_v, acc, hidden_v, down_v, held, sems = refs[7 + count :]
        copies = Copies(sems)
        loads = []
        for k in range(PARTS):
            at = slice(k * part, (k + 1) * part)
            loads.append(fetch_tokens(copies, place, [half.at[:, at] for half in latents], latents_v.at[:, at]))
            loads[k].append(copies.start(up.at[at], up_v.at[at]))
        if down is not None:
            later = [copies.start(down_hbm.at[:, pl.ds(k * part, part)], down_v.at[:, pl.ds(k * part, part)]) for k in range(PARTS)]
        squares = 0.0
        for k in range(PARTS):
            at = slice(k * part, (k + 1) * part)
            wait(loads[k])
            value = dot(up_v[at], latents_v[:, at], (0, 1))
            acc[...] = value if k == 0 else acc[...] + value
            floats = latents_v[:, at].astype(F32)
            squares = squares + jnp.sum(floats * floats, axis=1, keepdims=True)
        squares = jnp.broadcast_to(squares, (rows, 128)).T[:1]
        factor = lax.rsqrt(squares / width + 1e-06)
        scale[...] = factor
        values = acc[...] * factor
        acc[...] = values if down is not None else gelu_slope(values) * factor
        kept = [copies.start(acc, preact)]
        hidden_v[...] = smooth_gelu(values).astype(BF16)
        kept.append(copies.start(hidden_v, hidden))
        if down is not None:
            stores = []
            for k in range(PARTS):
                later[k].wait()
                value = dot(down_v[:, k * part : (k + 1) * part], hidden_v[...], (0, 0))
                stores += split_by_core(copies, place, block, value, out, held, k)
            wait(stores)
        wait(kept)

    scratch = [
        pltpu.VMEM((rows, width), BF16),
        pltpu.VMEM((width, inner), BF16),
        pltpu.VMEM((inner, rows), F32),
        pltpu.VMEM((inner, rows), BF16),
    ]
    if down is not None:
        scratch += [pltpu.VMEM((inner, width), BF16), held]
    out_shape = [
        jax.ShapeDtypeStruct((inner, rows), F32),
        jax.ShapeDtypeStruct((inner, rows), BF16),
        jax.ShapeDtypeStruct((1, rows), F32),
    ]
    vmem = pl.BlockSpec(memory_space=pltpu.VMEM)
    return pl.pallas_call(
        kernel,
        in_specs=[SMEM] + [HBM] * (halves + (1 if down is None else 2)),
        out_specs=[HBM, HBM, vmem] + ([] if down is None else [HBM] * count),
        out_shape=out_shape + ([] if down is None else sums),
        scratch_shapes=scratch + [pltpu.SemaphoreType.DMA((6 * PARTS + shards + 2,))],
        compiler_params=PARAMS,
        cost_estimate=pl.CostEstimate(flops=4 * rows * width * inner, bytes_accessed=6 * width * inner, transcendentals=rows * inner),
        name="student_forward",
    )(place, *latents, up, *([] if down is None else [down]))


def score(place, factor, pieces, layout, up, down, shards):
    width, inner = up.shape
    rows = pieces[0].shape[-1]
    block = width // shards
    part = width // PARTS
    count = len(pieces)
    sums, held = sum_shapes(shards, width, rows)

    def kernel(place, factor, *refs):
        pieces, refs = refs[:count], refs[count:]
        up, down = refs[:2]
        out = refs[2 : 2 + len(sums)]
        image, up_v, down_v, acc, active, held, sems = refs[2 + len(sums) :]
        copies = Copies(sems)
        loads = []
        for k in range(PARTS):
            at = slice(k * part, (k + 1) * part)
            loads.append(fetch_pieces(copies, place, pieces, layout, image, k, block) + [copies.start(up.at[at], up_v.at[at])])
        later = [copies.start(down.at[:, pl.ds(k * part, part)], down_v.at[:, pl.ds(k * part, part)]) for k in range(PARTS)]
        squares = 0.0
        for k in range(PARTS):
            at = slice(k * part, (k + 1) * part)
            wait(loads[k])
            value = dot(up_v[at], image[at], (0, 0))
            acc[...] = value if k == 0 else acc[...] + value
            floats = image[at].astype(F32)
            squares = squares + jnp.sum(floats * floats, axis=0, keepdims=True)
        scale = lax.rsqrt(squares / width + 1e-06)
        active[...] = smooth_gelu(acc[...] * scale).astype(BF16)
        stores = []
        for k in range(PARTS):
            later[k].wait()
            value = factor[0] * dot(down_v[:, k * part : (k + 1) * part], active[...], (0, 0))
            stores += split_by_core(copies, place, block, value, out, held, k)
        wait(stores)

    return pl.pallas_call(
        kernel,
        in_specs=[SMEM, SMEM] + [HBM] * (count + 2),
        out_specs=[HBM] * len(sums),
        out_shape=sums,
        scratch_shapes=[
            pltpu.VMEM((width, rows), BF16),
            pltpu.VMEM((width, inner), BF16),
            pltpu.VMEM((inner, width), BF16),
            pltpu.VMEM((inner, rows), F32),
            pltpu.VMEM((inner, rows), BF16),
            held,
            pltpu.SemaphoreType.DMA((4 * PARTS + 3 * shards,)),
        ],
        compiler_params=PARAMS,
        cost_estimate=pl.CostEstimate(flops=4 * rows * width * inner, bytes_accessed=6 * width * inner, transcendentals=rows * inner),
        name="score_member",
    )(place, factor, *pieces, up, down)


def inward_gradient(place, pieces, layout, down, slope, shards):
    inner, width = down.shape
    rows = slope.shape[1]
    part = width // PARTS
    count = len(pieces)

    def kernel(place, *refs):
        pieces, refs = refs[:count], refs[count:]
        down, slope, inward, image, down_v, acc = refs[:6]
        copies = Copies(refs[6])
        loads = []
        for k in range(PARTS):
            at = pl.ds(k * part, part)
            loads.append([copies.start(down.at[:, at], down_v.at[:, at])])
            loads[k] += fetch_pieces(copies, place, pieces, layout, image, k, width // shards)
        for k in range(PARTS):
            at = slice(k * part, (k + 1) * part)
            wait(loads[k])
            value = dot(down_v[:, at], image[at], (1, 0))
            acc[...] = value if k == 0 else acc[...] + value
        inward[...] = (acc[...] * slope[...]).astype(BF16)

    vmem = pl.BlockSpec(memory_space=pltpu.VMEM)
    return pl.pallas_call(
        kernel,
        in_specs=[SMEM] + [HBM] * (count + 1) + [vmem],
        out_specs=vmem,
        out_shape=jax.ShapeDtypeStruct((inner, rows), BF16),
        scratch_shapes=[
            pltpu.VMEM((width, rows), BF16),
            pltpu.VMEM((inner, width), BF16),
            pltpu.VMEM((inner, rows), F32),
            pltpu.SemaphoreType.DMA((PARTS + 2 * shards,)),
        ],
        compiler_params=PARAMS,
        cost_estimate=pl.CostEstimate(flops=2 * rows * width * inner, bytes_accessed=6 * width * inner, transcendentals=0),
        name="inward_gradient",
    )(place, *pieces, down, slope)


def weight_gradients(place, updates, layouts, down, slope, hiddens, tokens, inward, shards):
    inner, width = down.shape
    rows = slope.shape[1]
    block = width // shards
    part = width // PARTS
    counts = [len(pieces) for pieces in updates]
    halves = [len(t) for t in tokens]

    def kernel(place, *refs):
        refs = list(refs)

        def next_refs(number):
            taken = refs[:number]
            del refs[:number]
            return taken

        pieces = [next_refs(number) for number in counts]
        tokens = [next_refs(number) for number in halves]
        down, slope, first, second, before, grad_up, grad_down = next_refs(7)
        images, down_v, slope_v, hiddens_v, acc, inward_v, tokens_v, out_up, out_down, sems = refs
        copies = Copies(sems)

        def load(k):
            at = pl.ds(k * part, part)
            started = fetch_pieces(copies, place, pieces[1], layouts[1], images.at[:, pl.ds(rows, rows)], k, block)
            return started + [copies.start(down.at[:, at], down_v.at[:, at])]

        loads = [load(k) for k in range(PARTS)]
        late = [copies.start(slope, slope_v), copies.start(before, inward_v.at[:, pl.ds(0, rows)])]
        near = []
        for i in range(2):
            near += fetch_tokens(copies, place, tokens[i], tokens_v.at[pl.ds(i * rows, rows)])
        for k in range(PARTS):
            at = slice(k * part, (k + 1) * part)
            wait(loads[k])
            value = dot(down_v[:, at], images[at, rows:], (1, 0))
            acc[...] = value if k == 0 else acc[...] + value
        wait(late)
        inward_v[:, rows:] = (acc[...] * slope_v[...]).astype(BF16)
        far = [copies.start(first, hiddens_v.at[:, pl.ds(0, rows)]), copies.start(second, hiddens_v.at[:, pl.ds(rows, rows)])]
        for k in range(PARTS):
            far += fetch_pieces(copies, place, pieces[0], layouts[0], images.at[:, pl.ds(0, rows)], k, block)
        wait(near)
        stores = []
        for k in range(PARTS):
            at = slice(k * part, (k + 1) * part)
            out_up[k] = dot(tokens_v[:, at], inward_v[...], (0, 1))
            stores.append(copies.start(out_up.at[k], grad_up.at[pl.ds(k * part, part)]))
        wait(far)
        for k in range(PARTS):
            at = slice(k * part, (k + 1) * part)
            out_down[k] = dot(hiddens_v[...], images[at], (1, 1))
            stores.append(copies.start(out_down.at[k], grad_down.at[:, pl.ds(k * part, part)]))
        wait(stores)

    return pl.pallas_call(
        kernel,
        in_specs=[SMEM] + [HBM] * (sum(counts) + sum(halves) + 5),
        out_specs=[HBM] * 2,
        out_shape=[
            jax.ShapeDtypeStruct((width, inner), F32),
            jax.ShapeDtypeStruct((inner, width), F32),
        ],
        scratch_shapes=[
            pltpu.VMEM((width, 2 * rows), BF16),
            pltpu.VMEM((inner, width), BF16),
            pltpu.VMEM((inner, rows), F32),
            pltpu.VMEM((inner, 2 * rows), BF16),
            pltpu.VMEM((inner, rows), F32),
            pltpu.VMEM((inner, 2 * rows), BF16),
            pltpu.VMEM((2 * rows, width), BF16),
            pltpu.VMEM((PARTS, part, inner), F32),
            pltpu.VMEM((PARTS, inner, part), F32),
            pltpu.SemaphoreType.DMA((3 * PARTS + 10 + 4 * shards,)),
        ],
        compiler_params=PARAMS,
        cost_estimate=pl.CostEstimate(flops=10 * rows * width * inner, bytes_accessed=16 * width * inner, transcendentals=0),
        name="weight_gradients",
    )(place, *updates[0], *updates[1], *tokens[0], *tokens[1], down, slope, *hiddens, inward)


def make_body(roles, shards):
    devices = roles * shards
    depth = shards // 4
    ROLE, PAIR, CORE = shards, 2, 1
    columns = [[4 * k + low for k in range(depth)] for low in range(4)]

    def swap(value, mask):
        return lax.ppermute(value, AXES, [(i, i ^ mask) for i in range(devices)])

    def body(latents, fresh_noise, sigmas, student_up, student_down, score_up, score_down):
        rows, width = latents.shape
        block = width // shards
        role = lax.axis_index("role")
        index = lax.axis_index("tp")
        outer, pair, core = index // 4, (index // 2) % 2, index % 2
        place = jnp.stack([core, pair]).astype(jnp.int32)
        own_level = take(sigmas, role, 0)
        other_level = take(sigmas, 1 - role, 0)
        polarity = 1.0 - 2.0 * role.astype(F32)

        def outer_swaps(part, steps):
            return [swap(take(part, outer ^ k, 0), 4 * k) for k in steps]

        def outer_sum(part):
            return add(take(part, outer, 0), *outer_swaps(part, range(1, depth)))

        def student_sum(grid):
            cut = block // 3 // 16 * 16
            first, later = grid[:, :, :cut], grid[:, :, cut:]
            kept = add(take(later, pair, 1), swap(take(later, 1 - pair, 1), PAIR)).astype(BF16)
            later = outer_sum(kept)
            if not cut:
                return later
            kept = outer_sum(first).astype(BF16)
            first = add(take(kept, pair, 0), swap(take(kept, 1 - pair, 0), PAIR))
            return jnp.concatenate([first, later], axis=0)

        def gather(part, during):
            half = block // 2
            stack = lax.all_gather(part, "tp", axis_index_groups=columns, axis=0)
            by_pair = swap(stack, PAIR)
            by_role = swap(stack, ROLE)
            own = assemble((stack, by_pair, swap(stack, CORE), swap(by_pair, CORE)), OWN)
            by_both = [swap(by_role[:, :half], PAIR), swap(by_pair[:, half:], ROLE)]
            meanwhile = during(*own)
            by_both, meanwhile = lax.optimization_barrier((by_both, meanwhile))
            other = (by_role, *by_both, swap(by_role, CORE), *[swap(piece, CORE) for piece in by_both])
            return own, assemble(other, OTHER), meanwhile

        OWN = ((0, 0, 0), (1, 0, 0), (0, 1, 0), (1, 1, 0))
        OTHER = ((0, 0, 0), (1, 0, 0), (1, 0, block // 2), (0, 1, 0), (1, 1, 0), (1, 1, block // 2))

        def assemble(pieces, layout):
            if block % 32 == 0:
                return pieces, layout
            image = jnp.zeros((depth, 2, 2, block, rows), BF16)
            for piece, (row, column, first) in zip(pieces, layout):
                row = 1 - pair if row else pair
                column = 1 - core if column else core
                image = lax.dynamic_update_slice(image, piece[:, None, None], (0, row, column, first, 0))
            return (image.reshape(width, rows),), ()

        def core_sum(out):
            if len(out) == 1:
                grid = out[0].reshape(depth, 2, 2, block, rows)
                out = take(grid, 1 - core, 2), take(grid, core, 2)
            return add(out[1], swap(out[0], CORE)).astype(BF16).reshape(depth, 2, block, rows)

        def scatter(own, other, during):
            cut = block // 3 // 32 * 32
            rest = block - cut
            half = cut + rest // 2

            def planes(own, other, half):
                both, by_role = take(other, 1 - pair, 0), take(other, pair, 0)
                by_pair, kept = take(own, 1 - pair, 0), take(own, pair, 0)
                axis = both.ndim - 2
                low = lambda array: lax.slice_in_dim(array, 0, half, axis=axis)
                high = lambda array: lax.slice_in_dim(array, half, array.shape[axis], axis=axis)
                from_pair = swap(low(both), PAIR)
                from_role = swap(high(both), ROLE)
                by_role = jnp.concatenate([add(low(by_role), from_pair).astype(BF16), high(by_role)], axis=axis)
                by_pair = jnp.concatenate([low(by_pair), add(high(by_pair), from_role).astype(BF16)], axis=axis)
                return add(kept, swap(by_role, ROLE), swap(by_pair, PAIR)).astype(BF16)

            result = []
            if cut:
                images = jnp.stack([own[:, :, :cut], other[:, :, :cut]], axis=1)
                images = outer_sum(images).astype(BF16)
            kept = planes(own[:, :, cut:].swapaxes(0, 1), other[:, :, cut:].swapaxes(0, 1), rest // 2)
            if cut:
                kept, images = lax.optimization_barrier((kept, images))
                result.append(
                    add(
                        take(images[0], pair, 0),
                        swap(take(images[0], 1 - pair, 0), PAIR),
                        swap(take(images[1], pair, 0), ROLE),
                        swap(take(images[1], 1 - pair, 0), ROLE | PAIR),
                    )
                )
            result.append(outer_sum(kept))
            return jnp.concatenate(result, axis=0), during()

        share = rows // 2
        near = swap(lax.dynamic_slice_in_dim(latents, core * share, share, 0), ROLE)

        preact, hidden, scale, *out = student(place, (latents,), student_up, student_down, shards)
        made = student_sum(core_sum(out)).astype(BF16)
        noise = fresh_noise.T.astype(F32)
        blended = ((1.0 - own_level) * made.astype(F32) + own_level * noise).astype(BF16)
        slope = gelu_slope(preact) * scale
        blended, near, slope = lax.optimization_barrier((blended, near, slope))
        far = swap(near, CORE)

        def scored(pieces, layout, level):
            return score(place, (polarity * level)[None], pieces, layout, score_up[0], score_down[0], shards)

        _, (pieces, layout), out = gather(blended, lambda *own: scored(*own, own_level))
        tokens_other, out = lax.optimization_barrier(((near, far), out))
        own_sum = core_sum(out)
        other_sum = core_sum(scored(pieces, layout, other_level))

        def other_forward():
            slope_other, hidden_other, _ = student(place, tokens_other, student_up, None, shards)
            return hidden_other, slope_other

        update, (hidden_other, slope_other) = scatter(own_sum, other_sum, other_forward)
        update, hidden_other, slope_other = lax.optimization_barrier((update.astype(BF16), hidden_other, slope_other))
        (pieces, layout), (pieces_other, layout_other), inward = gather(
            update, lambda *own: inward_gradient(place, *own, student_down, slope, shards)
        )
        grad_up, grad_down = weight_gradients(
            place, (pieces, pieces_other), (layout, layout_other), student_down, slope_other,
            (hidden, hidden_other), ((latents,), tokens_other), inward, shards,
        )
        return (made.T, grad_up, grad_down)

    return body


def solution(mesh):
    return jax.shard_map(
        make_body(mesh.shape["role"], mesh.shape["tp"]),
        mesh=mesh,
        in_specs=(
            P("role", None),
            P("role", "tp"),
            P(),
            P(None, "tp"),
            P("tp", None),
            P("role", None, "tp"),
            P("role", "tp", None),
        ),
        out_specs=(P("role", "tp"), P(None, "tp"), P("tp", None)),
        check_vma=False,
    )
```

```python
import jax
import jax.numpy as jnp
from jax import lax
from jax.experimental import pallas as pl
from jax.experimental.pallas import tpu as pltpu
from jax.sharding import PartitionSpec as P

AXES = ("role", "tp")
BF16 = jnp.bfloat16
F32 = jnp.float32
PARTS = 4
SMEM = pl.BlockSpec(memory_space=pltpu.SMEM)
HBM = pl.BlockSpec(memory_space=pl.ANY)
PARAMS = pltpu.CompilerParams(vmem_limit_bytes=60 * 2**20)


def smooth_gelu(values):
    return jax.nn.gelu(values, approximate=True)


def gelu_slope(x):
    root, cubic = 0.7978845608028654, 0.044715
    bent = jnp.tanh(root * (x + cubic * x * x * x))
    return 0.5 * (1.0 + bent) + 0.5 * x * (1.0 - bent * bent) * root * (1.0 + 3.0 * cubic * x * x)


def dot(a, b, dims):
    return lax.dot_general(a, b, ((dims[:1], dims[1:]), ((), ())), preferred_element_type=F32)


def add(*terms):
    total = terms[0].astype(F32)
    for term in terms[1:]:
        total = total + term.astype(F32)
    return total


def take(array, index, axis):
    return lax.dynamic_index_in_dim(array, index, axis, keepdims=False)


class Copies:
    def __init__(self, sems):
        self.sems, self.used = sems, 0

    def start(self, source, target):
        copy = pltpu.make_async_copy(source, target, self.sems.at[self.used])
        self.used += 1
        copy.start()
        return copy


def wait(copies):
    for copy in copies:
        copy.wait()


def fetch_pieces(copies, place, pieces, layout, image, part, block):
    if not layout:
        height = image.shape[0] // PARTS
        at = pl.ds(part * height, height)
        return [copies.start(pieces[0].at[at], image.at[at])]
    core, pair = place[0], place[1]
    some = pieces[0].shape[0] // PARTS
    started = []
    for outer in range(part * some, (part + 1) * some):
        for piece, (row, column, first) in zip(pieces, layout):
            row = 1 - pair if row else pair
            column = 1 - core if column else core
            at = pl.multiple_of(((outer * 2 + row) * 2 + column) * block + first, 16)
            started.append(copies.start(piece.at[outer], image.at[pl.ds(at, piece.shape[1])]))
    return started


def fetch_tokens(copies, place, halves, tokens):
    if len(halves) == 1:
        return [copies.start(halves[0], tokens)]
    share = halves[0].shape[0]
    return [
        copies.start(half, tokens.at[pl.ds(pl.multiple_of(at * share, 16), share)])
        for half, at in zip(halves, (place[0], 1 - place[0]))
    ]


def split_by_core(copies, place, block, values, out, held, part):
    height = held.shape[1]
    if len(out) == 1:
        held[part] = values.astype(BF16)
        return [copies.start(held.at[part], out[0].at[pl.ds(part * height, height)])]
    core = place[0]
    held[part] = values.astype(BF16)
    pairs = height // (2 * block)
    started = []
    for p in range(pairs):
        for target, column in zip(out, (1 - core, core)):
            at = pl.multiple_of((2 * p + column) * block, 16)
            started.append(copies.start(held.at[part, pl.ds(at, block)], target.at[part * pairs + p]))
    return started


def sum_shapes(shards, width, rows):
    block = width // shards
    held = pltpu.VMEM((PARTS, width // PARTS, rows), BF16)
    if block % 16:
        return [jax.ShapeDtypeStruct((width, rows), BF16)], held
    piece = jax.ShapeDtypeStruct((shards // 2, block, rows), BF16)
    return [piece, piece], held


def student(place, latents, up, down, shards):
    rows = sum(half.shape[0] for half in latents)
    width, inner = up.shape
    block = width // shards
    part = width // PARTS
    halves = len(latents)
    sums, held = sum_shapes(shards, width, rows)
    count = len(sums)

    def kernel(*refs):
        place, latents, up = refs[0], refs[1 : 1 + halves], refs[1 + halves]
        refs = refs[halves - 1 :]
        if down is None:
            preact, hidden, scale, latents_v, up_v, acc, hidden_v, sems = refs[3:]
        else:
            down_hbm, preact, hidden, scale = refs[3:7]
            out = refs[7 : 7 + count]
            latents_v, up_v, acc, hidden_v, down_v, held, sems = refs[7 + count :]
        copies = Copies(sems)
        loads = []
        for k in range(PARTS):
            at = slice(k * part, (k + 1) * part)
            loads.append(fetch_tokens(copies, place, [half.at[:, at] for half in latents], latents_v.at[:, at]))
            loads[k].append(copies.start(up.at[at], up_v.at[at]))
        if down is not None:
            later = [copies.start(down_hbm.at[:, pl.ds(k * part, part)], down_v.at[:, pl.ds(k * part, part)]) for k in range(PARTS)]
        squares = 0.0
        for k in range(PARTS):
            at = slice(k * part, (k + 1) * part)
            wait(loads[k])
            value = dot(up_v[at], latents_v[:, at], (0, 1))
            acc[...] = value if k == 0 else acc[...] + value
            floats = latents_v[:, at].astype(F32)
            squares = squares + jnp.sum(floats * floats, axis=1, keepdims=True)
        squares = jnp.broadcast_to(squares, (rows, 128)).T[:1]
        factor = lax.rsqrt(squares / width + 1e-06)
        scale[...] = factor
        values = acc[...] * factor
        acc[...] = values if down is not None else gelu_slope(values) * factor
        kept = [copies.start(acc, preact)]
        hidden_v[...] = smooth_gelu(values).astype(BF16)
        kept.append(copies.start(hidden_v, hidden))
        if down is not None:
            stores = []
            for k in range(PARTS):
                later[k].wait()
                value = dot(down_v[:, k * part : (k + 1) * part], hidden_v[...], (0, 0))
                stores += split_by_core(copies, place, block, value, out, held, k)
            wait(stores)
        wait(kept)

    scratch = [
        pltpu.VMEM((rows, width), BF16),
        pltpu.VMEM((width, inner), BF16),
        pltpu.VMEM((inner, rows), F32),
        pltpu.VMEM((inner, rows), BF16),
    ]
    if down is not None:
        scratch += [pltpu.VMEM((inner, width), BF16), held]
    out_shape = [
        jax.ShapeDtypeStruct((inner, rows), F32),
        jax.ShapeDtypeStruct((inner, rows), BF16),
        jax.ShapeDtypeStruct((1, rows), F32),
    ]
    vmem = pl.BlockSpec(memory_space=pltpu.VMEM)
    return pl.pallas_call(
        kernel,
        in_specs=[SMEM] + [HBM] * (halves + (1 if down is None else 2)),
        out_specs=[HBM, HBM, vmem] + ([] if down is None else [HBM] * count),
        out_shape=out_shape + ([] if down is None else sums),
        scratch_shapes=scratch + [pltpu.SemaphoreType.DMA((6 * PARTS + shards + 2,))],
        compiler_params=PARAMS,
        cost_estimate=pl.CostEstimate(flops=4 * rows * width * inner, bytes_accessed=6 * width * inner, transcendentals=rows * inner),
        name="student_forward",
    )(place, *latents, up, *([] if down is None else [down]))


def score(place, factor, pieces, layout, up, down, shards):
    width, inner = up.shape
    rows = pieces[0].shape[-1]
    block = width // shards
    part = width // PARTS
    count = len(pieces)
    sums, held = sum_shapes(shards, width, rows)

    def kernel(place, factor, *refs):
        pieces, refs = refs[:count], refs[count:]
        up, down = refs[:2]
        out = refs[2 : 2 + len(sums)]
        image, up_v, down_v, acc, active, held, sems = refs[2 + len(sums) :]
        copies = Copies(sems)
        loads = []
        for k in range(PARTS):
            at = slice(k * part, (k + 1) * part)
            loads.append(fetch_pieces(copies, place, pieces, layout, image, k, block) + [copies.start(up.at[at], up_v.at[at])])
        later = [copies.start(down.at[:, pl.ds(k * part, part)], down_v.at[:, pl.ds(k * part, part)]) for k in range(PARTS)]
        squares = 0.0
        for k in range(PARTS):
            at = slice(k * part, (k + 1) * part)
            wait(loads[k])
            value = dot(up_v[at], image[at], (0, 0))
            acc[...] = value if k == 0 else acc[...] + value
            floats = image[at].astype(F32)
            squares = squares + jnp.sum(floats * floats, axis=0, keepdims=True)
        scale = lax.rsqrt(squares / width + 1e-06)
        active[...] = smooth_gelu(acc[...] * scale).astype(BF16)
        stores = []
        for k in range(PARTS):
            later[k].wait()
            value = factor[0] * dot(down_v[:, k * part : (k + 1) * part], active[...], (0, 0))
            stores += split_by_core(copies, place, block, value, out, held, k)
        wait(stores)

    return pl.pallas_call(
        kernel,
        in_specs=[SMEM, SMEM] + [HBM] * (count + 2),
        out_specs=[HBM] * len(sums),
        out_shape=sums,
        scratch_shapes=[
            pltpu.VMEM((width, rows), BF16),
            pltpu.VMEM((width, inner), BF16),
            pltpu.VMEM((inner, width), BF16),
            pltpu.VMEM((inner, rows), F32),
            pltpu.VMEM((inner, rows), BF16),
            held,
            pltpu.SemaphoreType.DMA((4 * PARTS + 3 * shards,)),
        ],
        compiler_params=PARAMS,
        cost_estimate=pl.CostEstimate(flops=4 * rows * width * inner, bytes_accessed=6 * width * inner, transcendentals=rows * inner),
        name="score_member",
    )(place, factor, *pieces, up, down)


def inward_gradient(place, pieces, layout, down, slope, shards):
    inner, width = down.shape
    rows = slope.shape[1]
    part = width // PARTS
    count = len(pieces)

    def kernel(place, *refs):
        pieces, refs = refs[:count], refs[count:]
        down, slope, inward, image, down_v, acc = refs[:6]
        copies = Copies(refs[6])
        loads = []
        for k in range(PARTS):
            at = pl.ds(k * part, part)
            loads.append([copies.start(down.at[:, at], down_v.at[:, at])])
            loads[k] += fetch_pieces(copies, place, pieces, layout, image, k, width // shards)
        for k in range(PARTS):
            at = slice(k * part, (k + 1) * part)
            wait(loads[k])
            value = dot(down_v[:, at], image[at], (1, 0))
            acc[...] = value if k == 0 else acc[...] + value
        inward[...] = (acc[...] * slope[...]).astype(BF16)

    vmem = pl.BlockSpec(memory_space=pltpu.VMEM)
    return pl.pallas_call(
        kernel,
        in_specs=[SMEM] + [HBM] * (count + 1) + [vmem],
        out_specs=vmem,
        out_shape=jax.ShapeDtypeStruct((inner, rows), BF16),
        scratch_shapes=[
            pltpu.VMEM((width, rows), BF16),
            pltpu.VMEM((inner, width), BF16),
            pltpu.VMEM((inner, rows), F32),
            pltpu.SemaphoreType.DMA((PARTS + 2 * shards,)),
        ],
        compiler_params=PARAMS,
        cost_estimate=pl.CostEstimate(flops=2 * rows * width * inner, bytes_accessed=6 * width * inner, transcendentals=0),
        name="inward_gradient",
    )(place, *pieces, down, slope)


def weight_gradients(place, updates, layouts, down, slope, hiddens, tokens, inward, shards):
    inner, width = down.shape
    rows = slope.shape[1]
    block = width // shards
    part = width // PARTS
    counts = [len(pieces) for pieces in updates]
    halves = [len(t) for t in tokens]

    def kernel(place, *refs):
        refs = list(refs)

        def next_refs(number):
            taken = refs[:number]
            del refs[:number]
            return taken

        pieces = [next_refs(number) for number in counts]
        tokens = [next_refs(number) for number in halves]
        down, slope, first, second, before, grad_up, grad_down = next_refs(7)
        images, down_v, slope_v, hiddens_v, acc, inward_v, tokens_v, out_up, out_down, sems = refs
        copies = Copies(sems)

        def load(k):
            at = pl.ds(k * part, part)
            started = fetch_pieces(copies, place, pieces[1], layouts[1], images.at[:, pl.ds(rows, rows)], k, block)
            return started + [copies.start(down.at[:, at], down_v.at[:, at])]

        loads = [load(k) for k in range(PARTS)]
        late = [copies.start(slope, slope_v), copies.start(before, inward_v.at[:, pl.ds(0, rows)])]
        near = []
        for i in range(2):
            near += fetch_tokens(copies, place, tokens[i], tokens_v.at[pl.ds(i * rows, rows)])
        for k in range(PARTS):
            at = slice(k * part, (k + 1) * part)
            wait(loads[k])
            value = dot(down_v[:, at], images[at, rows:], (1, 0))
            acc[...] = value if k == 0 else acc[...] + value
        wait(late)
        inward_v[:, rows:] = (acc[...] * slope_v[...]).astype(BF16)
        far = [copies.start(first, hiddens_v.at[:, pl.ds(0, rows)]), copies.start(second, hiddens_v.at[:, pl.ds(rows, rows)])]
        for k in range(PARTS):
            far += fetch_pieces(copies, place, pieces[0], layouts[0], images.at[:, pl.ds(0, rows)], k, block)
        wait(near)
        stores = []
        for k in range(PARTS):
            at = slice(k * part, (k + 1) * part)
            out_up[k] = dot(tokens_v[:, at], inward_v[...], (0, 1))
            stores.append(copies.start(out_up.at[k], grad_up.at[pl.ds(k * part, part)]))
        wait(far)
        for k in range(PARTS):
            at = slice(k * part, (k + 1) * part)
            out_down[k] = dot(hiddens_v[...], images[at], (1, 1))
            stores.append(copies.start(out_down.at[k], grad_down.at[:, pl.ds(k * part, part)]))
        wait(stores)

    return pl.pallas_call(
        kernel,
        in_specs=[SMEM] + [HBM] * (sum(counts) + sum(halves) + 5),
        out_specs=[HBM] * 2,
        out_shape=[
            jax.ShapeDtypeStruct((width, inner), F32),
            jax.ShapeDtypeStruct((inner, width), F32),
        ],
        scratch_shapes=[
            pltpu.VMEM((width, 2 * rows), BF16),
            pltpu.VMEM((inner, width), BF16),
            pltpu.VMEM((inner, rows), F32),
            pltpu.VMEM((inner, 2 * rows), BF16),
            pltpu.VMEM((inner, rows), F32),
            pltpu.VMEM((inner, 2 * rows), BF16),
            pltpu.VMEM((2 * rows, width), BF16),
            pltpu.VMEM((PARTS, part, inner), F32),
            pltpu.VMEM((PARTS, inner, part), F32),
            pltpu.SemaphoreType.DMA((3 * PARTS + 10 + 4 * shards,)),
        ],
        compiler_params=PARAMS,
        cost_estimate=pl.CostEstimate(flops=10 * rows * width * inner, bytes_accessed=16 * width * inner, transcendentals=0),
        name="weight_gradients",
    )(place, *updates[0], *updates[1], *tokens[0], *tokens[1], down, slope, *hiddens, inward)


def make_body(roles, shards):
    devices = roles * shards
    depth = shards // 4
    ROLE, PAIR, CORE = shards, 2, 1
    columns = [[4 * k + low for k in range(depth)] for low in range(4)]

    def swap(value, mask):
        return lax.ppermute(value, AXES, [(i, i ^ mask) for i in range(devices)])

    def body(latents, fresh_noise, sigmas, student_up, student_down, score_up, score_down):
        rows, width = latents.shape
        block = width // shards
        role = lax.axis_index("role")
        index = lax.axis_index("tp")
        outer, pair, core = index // 4, (index // 2) % 2, index % 2
        place = jnp.stack([core, pair]).astype(jnp.int32)
        own_level = take(sigmas, role, 0)
        other_level = take(sigmas, 1 - role, 0)
        polarity = 1.0 - 2.0 * role.astype(F32)

        def outer_swaps(part, steps):
            return [swap(take(part, outer ^ k, 0), 4 * k) for k in steps]

        def outer_sum(part):
            return add(take(part, outer, 0), *outer_swaps(part, range(1, depth)))

        def student_sum(grid):
            cut = block // 3 // 16 * 16
            first, later = grid[:, :, :cut], grid[:, :, cut:]
            kept = add(take(later, pair, 1), swap(take(later, 1 - pair, 1), PAIR)).astype(BF16)
            later = outer_sum(kept)
            if not cut:
                return later
            kept = outer_sum(first).astype(BF16)
            first = add(take(kept, pair, 0), swap(take(kept, 1 - pair, 0), PAIR))
            return jnp.concatenate([first, later], axis=0)

        def gather(part, during):
            half = block // 2
            stack = lax.all_gather(part, "tp", axis_index_groups=columns, axis=0)
            by_pair = swap(stack, PAIR)
            by_role = swap(stack, ROLE)
            own = assemble((stack, by_pair, swap(stack, CORE), swap(by_pair, CORE)), OWN)
            by_both = [swap(by_role[:, :half], PAIR), swap(by_pair[:, half:], ROLE)]
            meanwhile = during(*own)
            by_both, meanwhile = lax.optimization_barrier((by_both, meanwhile))
            other = (by_role, *by_both, swap(by_role, CORE), *[swap(piece, CORE) for piece in by_both])
            return own, assemble(other, OTHER), meanwhile

        OWN = ((0, 0, 0), (1, 0, 0), (0, 1, 0), (1, 1, 0))
        OTHER = ((0, 0, 0), (1, 0, 0), (1, 0, block // 2), (0, 1, 0), (1, 1, 0), (1, 1, block // 2))

        def assemble(pieces, layout):
            if block % 32 == 0:
                return pieces, layout
            image = jnp.zeros((depth, 2, 2, block, rows), BF16)
            for piece, (row, column, first) in zip(pieces, layout):
                row = 1 - pair if row else pair
                column = 1 - core if column else core
                image = lax.dynamic_update_slice(image, piece[:, None, None], (0, row, column, first, 0))
            return (image.reshape(width, rows),), ()

        def core_sum(out):
            if len(out) == 1:
                grid = out[0].reshape(depth, 2, 2, block, rows)
                out = take(grid, 1 - core, 2), take(grid, core, 2)
            return add(out[1], swap(out[0], CORE)).astype(BF16).reshape(depth, 2, block, rows)

        def scatter(own, other, during):
            cut = block // 4 // 16 * 16
            rest = block - cut
            half = cut + rest // 2

            def planes(own, other, half):
                both, by_role = take(other, 1 - pair, 0), take(other, pair, 0)
                by_pair, kept = take(own, 1 - pair, 0), take(own, pair, 0)
                axis = both.ndim - 2
                low = lambda array: lax.slice_in_dim(array, 0, half, axis=axis)
                high = lambda array: lax.slice_in_dim(array, half, array.shape[axis], axis=axis)
                from_pair = swap(low(both), PAIR)
                from_role = swap(high(both), ROLE)
                by_role = jnp.concatenate([add(low(by_role), from_pair).astype(BF16), high(by_role)], axis=axis)
                by_pair = jnp.concatenate([low(by_pair), add(high(by_pair), from_role).astype(BF16)], axis=axis)
                return add(kept, swap(by_role, ROLE), swap(by_pair, PAIR)).astype(BF16)

            result = []
            if cut:
                images = jnp.stack([own[:, :, :cut], other[:, :, :cut]], axis=1)
                images = outer_sum(images).astype(BF16)
            kept = planes(own[:, :, cut:].swapaxes(0, 1), other[:, :, cut:].swapaxes(0, 1), rest // 2)
            if cut:
                kept, images = lax.optimization_barrier((kept, images))
                result.append(
                    add(
                        take(images[0], pair, 0),
                        swap(take(images[0], 1 - pair, 0), PAIR),
                        swap(take(images[1], pair, 0), ROLE),
                        swap(take(images[1], 1 - pair, 0), ROLE | PAIR),
                    )
                )
            result.append(outer_sum(kept))
            return jnp.concatenate(result, axis=0), during()

        share = rows // 2
        near = swap(lax.dynamic_slice_in_dim(latents, core * share, share, 0), ROLE)

        preact, hidden, scale, *out = student(place, (latents,), student_up, student_down, shards)
        made = student_sum(core_sum(out)).astype(BF16)
        noise = fresh_noise.T.astype(F32)
        blended = ((1.0 - own_level) * made.astype(F32) + own_level * noise).astype(BF16)
        slope = gelu_slope(preact) * scale
        blended, near, slope = lax.optimization_barrier((blended, near, slope))
        far = swap(near, CORE)

        def scored(pieces, layout, level):
            return score(place, (polarity * level)[None], pieces, layout, score_up[0], score_down[0], shards)

        _, (pieces, layout), out = gather(blended, lambda *own: scored(*own, own_level))
        tokens_other, out = lax.optimization_barrier(((near, far), out))
        own_sum = core_sum(out)
        other_sum = core_sum(scored(pieces, layout, other_level))

        def other_forward():
            slope_other, hidden_other, _ = student(place, tokens_other, student_up, None, shards)
            return hidden_other, slope_other

        update, (hidden_other, slope_other) = scatter(own_sum, other_sum, other_forward)
        update, hidden_other, slope_other = lax.optimization_barrier((update.astype(BF16), hidden_other, slope_other))
        (pieces, layout), (pieces_other, layout_other), inward = gather(
            update, lambda *own: inward_gradient(place, *own, student_down, slope, shards)
        )
        grad_up, grad_down = weight_gradients(
            place, (pieces, pieces_other), (layout, layout_other), student_down, slope_other,
            (hidden, hidden_other), ((latents,), tokens_other), inward, shards,
        )
        return (made.T, grad_up, grad_down)

    return body


def solution(mesh):
    return jax.shard_map(
        make_body(mesh.shape["role"], mesh.shape["tp"]),
        mesh=mesh,
        in_specs=(
            P("role", None),
            P("role", "tp"),
            P(),
            P(None, "tp"),
            P("tp", None),
            P("role", None, "tp"),
            P("role", "tp", None),
        ),
        out_specs=(P("role", "tp"), P(None, "tp"), P("tp", None)),
        check_vma=False,
    )
```

```python
import jax
import jax.numpy as jnp
from jax import lax
from jax.experimental import pallas as pl
from jax.experimental.pallas import tpu as pltpu
from jax.sharding import PartitionSpec as P

AXES = ("role", "tp")
BF16 = jnp.bfloat16
F32 = jnp.float32
PARTS = 4
SMEM = pl.BlockSpec(memory_space=pltpu.SMEM)
HBM = pl.BlockSpec(memory_space=pl.ANY)
PARAMS = pltpu.CompilerParams(vmem_limit_bytes=60 * 2**20)


def smooth_gelu(values):
    return jax.nn.gelu(values, approximate=True)


def gelu_slope(x):
    root, cubic = 0.7978845608028654, 0.044715
    bent = jnp.tanh(root * (x + cubic * x * x * x))
    return 0.5 * (1.0 + bent) + 0.5 * x * (1.0 - bent * bent) * root * (1.0 + 3.0 * cubic * x * x)


def dot(a, b, dims):
    return lax.dot_general(a, b, ((dims[:1], dims[1:]), ((), ())), preferred_element_type=F32)


def add(*terms):
    total = terms[0].astype(F32)
    for term in terms[1:]:
        total = total + term.astype(F32)
    return total


def take(array, index, axis):
    return lax.dynamic_index_in_dim(array, index, axis, keepdims=False)


class Copies:
    def __init__(self, sems):
        self.sems, self.used = sems, 0

    def start(self, source, target):
        copy = pltpu.make_async_copy(source, target, self.sems.at[self.used])
        self.used += 1
        copy.start()
        return copy


def wait(copies):
    for copy in copies:
        copy.wait()


def fetch_pieces(copies, place, pieces, layout, image, part, block):
    if not layout:
        height = image.shape[0] // PARTS
        at = pl.ds(part * height, height)
        return [copies.start(pieces[0].at[at], image.at[at])]
    core, pair = place[0], place[1]
    some = pieces[0].shape[0] // PARTS
    started = []
    for outer in range(part * some, (part + 1) * some):
        for piece, (row, column, first) in zip(pieces, layout):
            row = 1 - pair if row else pair
            column = 1 - core if column else core
            at = pl.multiple_of(((outer * 2 + row) * 2 + column) * block + first, 16)
            started.append(copies.start(piece.at[outer], image.at[pl.ds(at, piece.shape[1])]))
    return started


def fetch_tokens(copies, place, halves, tokens):
    if len(halves) == 1:
        return [copies.start(halves[0], tokens)]
    share = halves[0].shape[0]
    return [
        copies.start(half, tokens.at[pl.ds(pl.multiple_of(at * share, 16), share)])
        for half, at in zip(halves, (place[0], 1 - place[0]))
    ]


def split_by_core(copies, place, block, values, out, held, part):
    height = held.shape[1]
    if len(out) == 1:
        held[part] = values.astype(BF16)
        return [copies.start(held.at[part], out[0].at[pl.ds(part * height, height)])]
    core = place[0]
    held[part] = values.astype(BF16)
    pairs = height // (2 * block)
    started = []
    for p in range(pairs):
        for target, column in zip(out, (1 - core, core)):
            at = pl.multiple_of((2 * p + column) * block, 16)
            started.append(copies.start(held.at[part, pl.ds(at, block)], target.at[part * pairs + p]))
    return started


def sum_shapes(shards, width, rows):
    block = width // shards
    held = pltpu.VMEM((PARTS, width // PARTS, rows), BF16)
    if block % 16:
        return [jax.ShapeDtypeStruct((width, rows), BF16)], held
    piece = jax.ShapeDtypeStruct((shards // 2, block, rows), BF16)
    return [piece, piece], held


def student(place, latents, up, down, shards):
    rows = sum(half.shape[0] for half in latents)
    width, inner = up.shape
    block = width // shards
    part = width // PARTS
    halves = len(latents)
    sums, held = sum_shapes(shards, width, rows)
    count = len(sums)

    def kernel(*refs):
        place, latents, up = refs[0], refs[1 : 1 + halves], refs[1 + halves]
        refs = refs[halves - 1 :]
        if down is None:
            preact, hidden, scale, latents_v, up_v, acc, hidden_v, sems = refs[3:]
        else:
            down_hbm, preact, hidden, scale = refs[3:7]
            out = refs[7 : 7 + count]
            latents_v, up_v, acc, hidden_v, down_v, held, sems = refs[7 + count :]
        copies = Copies(sems)
        loads = []
        for k in range(PARTS):
            at = slice(k * part, (k + 1) * part)
            loads.append(fetch_tokens(copies, place, [half.at[:, at] for half in latents], latents_v.at[:, at]))
            loads[k].append(copies.start(up.at[at], up_v.at[at]))
        if down is not None:
            later = [copies.start(down_hbm.at[:, pl.ds(k * part, part)], down_v.at[:, pl.ds(k * part, part)]) for k in range(PARTS)]
        squares = 0.0
        for k in range(PARTS):
            at = slice(k * part, (k + 1) * part)
            wait(loads[k])
            value = dot(up_v[at], latents_v[:, at], (0, 1))
            acc[...] = value if k == 0 else acc[...] + value
            floats = latents_v[:, at].astype(F32)
            squares = squares + jnp.sum(floats * floats, axis=1, keepdims=True)
        squares = jnp.broadcast_to(squares, (rows, 128)).T[:1]
        factor = lax.rsqrt(squares / width + 1e-06)
        scale[...] = factor
        values = acc[...] * factor
        acc[...] = values if down is not None else gelu_slope(values) * factor
        kept = [copies.start(acc, preact)]
        hidden_v[...] = smooth_gelu(values).astype(BF16)
        kept.append(copies.start(hidden_v, hidden))
        if down is not None:
            stores = []
            for k in range(PARTS):
                later[k].wait()
                value = dot(down_v[:, k * part : (k + 1) * part], hidden_v[...], (0, 0))
                stores += split_by_core(copies, place, block, value, out, held, k)
            wait(stores)
        wait(kept)

    scratch = [
        pltpu.VMEM((rows, width), BF16),
        pltpu.VMEM((width, inner), BF16),
        pltpu.VMEM((inner, rows), F32),
        pltpu.VMEM((inner, rows), BF16),
    ]
    if down is not None:
        scratch += [pltpu.VMEM((inner, width), BF16), held]
    out_shape = [
        jax.ShapeDtypeStruct((inner, rows), F32),
        jax.ShapeDtypeStruct((inner, rows), BF16),
        jax.ShapeDtypeStruct((1, rows), F32),
    ]
    vmem = pl.BlockSpec(memory_space=pltpu.VMEM)
    return pl.pallas_call(
        kernel,
        in_specs=[SMEM] + [HBM] * (halves + (1 if down is None else 2)),
        out_specs=[HBM, HBM, vmem] + ([] if down is None else [HBM] * count),
        out_shape=out_shape + ([] if down is None else sums),
        scratch_shapes=scratch + [pltpu.SemaphoreType.DMA((6 * PARTS + shards + 2,))],
        compiler_params=PARAMS,
        cost_estimate=pl.CostEstimate(flops=4 * rows * width * inner, bytes_accessed=6 * width * inner, transcendentals=rows * inner),
        name="student_forward",
    )(place, *latents, up, *([] if down is None else [down]))


def score(place, factor, pieces, layout, up, down, shards):
    width, inner = up.shape
    rows = pieces[0].shape[-1]
    block = width // shards
    part = width // PARTS
    count = len(pieces)
    sums, held = sum_shapes(shards, width, rows)

    def kernel(place, factor, *refs):
        pieces, refs = refs[:count], refs[count:]
        up, down = refs[:2]
        out = refs[2 : 2 + len(sums)]
        image, up_v, down_v, acc, active, held, sems = refs[2 + len(sums) :]
        copies = Copies(sems)
        loads = []
        for k in range(PARTS):
            at = slice(k * part, (k + 1) * part)
            loads.append(fetch_pieces(copies, place, pieces, layout, image, k, block) + [copies.start(up.at[at], up_v.at[at])])
        later = [copies.start(down.at[:, pl.ds(k * part, part)], down_v.at[:, pl.ds(k * part, part)]) for k in range(PARTS)]
        squares = 0.0
        for k in range(PARTS):
            at = slice(k * part, (k + 1) * part)
            wait(loads[k])
            value = dot(up_v[at], image[at], (0, 0))
            acc[...] = value if k == 0 else acc[...] + value
            floats = image[at].astype(F32)
            squares = squares + jnp.sum(floats * floats, axis=0, keepdims=True)
        scale = lax.rsqrt(squares / width + 1e-06)
        active[...] = smooth_gelu(acc[...] * scale).astype(BF16)
        stores = []
        for k in range(PARTS):
            later[k].wait()
            value = factor[0] * dot(down_v[:, k * part : (k + 1) * part], active[...], (0, 0))
            stores += split_by_core(copies, place, block, value, out, held, k)
        wait(stores)

    return pl.pallas_call(
        kernel,
        in_specs=[SMEM, SMEM] + [HBM] * (count + 2),
        out_specs=[HBM] * len(sums),
        out_shape=sums,
        scratch_shapes=[
            pltpu.VMEM((width, rows), BF16),
            pltpu.VMEM((width, inner), BF16),
            pltpu.VMEM((inner, width), BF16),
            pltpu.VMEM((inner, rows), F32),
            pltpu.VMEM((inner, rows), BF16),
            held,
            pltpu.SemaphoreType.DMA((4 * PARTS + 3 * shards,)),
        ],
        compiler_params=PARAMS,
        cost_estimate=pl.CostEstimate(flops=4 * rows * width * inner, bytes_accessed=6 * width * inner, transcendentals=rows * inner),
        name="score_member",
    )(place, factor, *pieces, up, down)


def inward_gradient(place, pieces, layout, down, slope, shards):
    inner, width = down.shape
    rows = slope.shape[1]
    part = width // PARTS
    count = len(pieces)

    def kernel(place, *refs):
        pieces, refs = refs[:count], refs[count:]
        down, slope, inward, image, down_v, acc = refs[:6]
        copies = Copies(refs[6])
        loads = []
        for k in range(PARTS):
            at = pl.ds(k * part, part)
            loads.append([copies.start(down.at[:, at], down_v.at[:, at])])
            loads[k] += fetch_pieces(copies, place, pieces, layout, image, k, width // shards)
        for k in range(PARTS):
            at = slice(k * part, (k + 1) * part)
            wait(loads[k])
            value = dot(down_v[:, at], image[at], (1, 0))
            acc[...] = value if k == 0 else acc[...] + value
        inward[...] = (acc[...] * slope[...]).astype(BF16)

    vmem = pl.BlockSpec(memory_space=pltpu.VMEM)
    return pl.pallas_call(
        kernel,
        in_specs=[SMEM] + [HBM] * (count + 1) + [vmem],
        out_specs=vmem,
        out_shape=jax.ShapeDtypeStruct((inner, rows), BF16),
        scratch_shapes=[
            pltpu.VMEM((width, rows), BF16),
            pltpu.VMEM((inner, width), BF16),
            pltpu.VMEM((inner, rows), F32),
            pltpu.SemaphoreType.DMA((PARTS + 2 * shards,)),
        ],
        compiler_params=PARAMS,
        cost_estimate=pl.CostEstimate(flops=2 * rows * width * inner, bytes_accessed=6 * width * inner, transcendentals=0),
        name="inward_gradient",
    )(place, *pieces, down, slope)


def weight_gradients(place, updates, layouts, down, slope, hiddens, tokens, inward, shards):
    inner, width = down.shape
    rows = slope.shape[1]
    block = width // shards
    part = width // PARTS
    counts = [len(pieces) for pieces in updates]
    halves = [len(t) for t in tokens]

    def kernel(place, *refs):
        refs = list(refs)

        def next_refs(number):
            taken = refs[:number]
            del refs[:number]
            return taken

        pieces = [next_refs(number) for number in counts]
        tokens = [next_refs(number) for number in halves]
        down, slope, first, second, before, grad_up, grad_down = next_refs(7)
        images, down_v, slope_v, hiddens_v, acc, inward_v, tokens_v, out_up, out_down, sems = refs
        copies = Copies(sems)

        def load(k):
            at = pl.ds(k * part, part)
            started = fetch_pieces(copies, place, pieces[1], layouts[1], images.at[:, pl.ds(rows, rows)], k, block)
            return started + [copies.start(down.at[:, at], down_v.at[:, at])]

        loads = [load(k) for k in range(PARTS)]
        late = [copies.start(slope, slope_v), copies.start(before, inward_v.at[:, pl.ds(0, rows)])]
        near = []
        for i in range(2):
            near += fetch_tokens(copies, place, tokens[i], tokens_v.at[pl.ds(i * rows, rows)])
        for k in range(PARTS):
            at = slice(k * part, (k + 1) * part)
            wait(loads[k])
            value = dot(down_v[:, at], images[at, rows:], (1, 0))
            acc[...] = value if k == 0 else acc[...] + value
        wait(late)
        inward_v[:, rows:] = (acc[...] * slope_v[...]).astype(BF16)
        far = [copies.start(first, hiddens_v.at[:, pl.ds(0, rows)]), copies.start(second, hiddens_v.at[:, pl.ds(rows, rows)])]
        for k in range(PARTS):
            far += fetch_pieces(copies, place, pieces[0], layouts[0], images.at[:, pl.ds(0, rows)], k, block)
        wait(near)
        stores = []
        for k in range(PARTS):
            at = slice(k * part, (k + 1) * part)
            out_up[k] = dot(tokens_v[:, at], inward_v[...], (0, 1))
            stores.append(copies.start(out_up.at[k], grad_up.at[pl.ds(k * part, part)]))
        wait(far)
        for k in range(PARTS):
            at = slice(k * part, (k + 1) * part)
            out_down[k] = dot(hiddens_v[...], images[at], (1, 1))
            stores.append(copies.start(out_down.at[k], grad_down.at[:, pl.ds(k * part, part)]))
        wait(stores)

    return pl.pallas_call(
        kernel,
        in_specs=[SMEM] + [HBM] * (sum(counts) + sum(halves) + 5),
        out_specs=[HBM] * 2,
        out_shape=[
            jax.ShapeDtypeStruct((width, inner), F32),
            jax.ShapeDtypeStruct((inner, width), F32),
        ],
        scratch_shapes=[
            pltpu.VMEM((width, 2 * rows), BF16),
            pltpu.VMEM((inner, width), BF16),
            pltpu.VMEM((inner, rows), F32),
            pltpu.VMEM((inner, 2 * rows), BF16),
            pltpu.VMEM((inner, rows), F32),
            pltpu.VMEM((inner, 2 * rows), BF16),
            pltpu.VMEM((2 * rows, width), BF16),
            pltpu.VMEM((PARTS, part, inner), F32),
            pltpu.VMEM((PARTS, inner, part), F32),
            pltpu.SemaphoreType.DMA((3 * PARTS + 10 + 4 * shards,)),
        ],
        compiler_params=PARAMS,
        cost_estimate=pl.CostEstimate(flops=10 * rows * width * inner, bytes_accessed=16 * width * inner, transcendentals=0),
        name="weight_gradients",
    )(place, *updates[0], *updates[1], *tokens[0], *tokens[1], down, slope, *hiddens, inward)


def make_body(roles, shards):
    devices = roles * shards
    depth = shards // 4
    ROLE, PAIR, CORE = shards, 2, 1
    columns = [[4 * k + low for k in range(depth)] for low in range(4)]

    def swap(value, mask):
        return lax.ppermute(value, AXES, [(i, i ^ mask) for i in range(devices)])

    def body(latents, fresh_noise, sigmas, student_up, student_down, score_up, score_down):
        rows, width = latents.shape
        block = width // shards
        role = lax.axis_index("role")
        index = lax.axis_index("tp")
        outer, pair, core = index // 4, (index // 2) % 2, index % 2
        place = jnp.stack([core, pair]).astype(jnp.int32)
        own_level = take(sigmas, role, 0)
        other_level = take(sigmas, 1 - role, 0)
        polarity = 1.0 - 2.0 * role.astype(F32)

        def outer_swaps(part, steps):
            return [swap(take(part, outer ^ k, 0), 4 * k) for k in steps]

        def outer_sum(part):
            return add(take(part, outer, 0), *outer_swaps(part, range(1, depth)))

        def student_sum(grid):
            cut = block // 3 // 16 * 16
            first, later = grid[:, :, :cut], grid[:, :, cut:]
            kept = add(take(later, pair, 1), swap(take(later, 1 - pair, 1), PAIR)).astype(BF16)
            later = outer_sum(kept)
            if not cut:
                return later
            kept = outer_sum(first).astype(BF16)
            first = add(take(kept, pair, 0), swap(take(kept, 1 - pair, 0), PAIR))
            return jnp.concatenate([first, later], axis=0)

        def gather(part, during):
            half = block // 2
            stack = lax.all_gather(part, "tp", axis_index_groups=columns, axis=0)
            by_pair = swap(stack, PAIR)
            by_role = swap(stack, ROLE)
            own = assemble((stack, by_pair, swap(stack, CORE), swap(by_pair, CORE)), OWN)
            by_both = [swap(by_role[:, :half], PAIR), swap(by_pair[:, half:], ROLE)]
            meanwhile = during(*own)
            by_both, meanwhile = lax.optimization_barrier((by_both, meanwhile))
            other = (by_role, *by_both, swap(by_role, CORE), *[swap(piece, CORE) for piece in by_both])
            return own, assemble(other, OTHER), meanwhile

        OWN = ((0, 0, 0), (1, 0, 0), (0, 1, 0), (1, 1, 0))
        OTHER = ((0, 0, 0), (1, 0, 0), (1, 0, block // 2), (0, 1, 0), (1, 1, 0), (1, 1, block // 2))

        def assemble(pieces, layout):
            if block % 32 == 0:
                return pieces, layout
            image = jnp.zeros((depth, 2, 2, block, rows), BF16)
            for piece, (row, column, first) in zip(pieces, layout):
                row = 1 - pair if row else pair
                column = 1 - core if column else core
                image = lax.dynamic_update_slice(image, piece[:, None, None], (0, row, column, first, 0))
            return (image.reshape(width, rows),), ()

        def core_sum(out):
            if len(out) == 1:
                grid = out[0].reshape(depth, 2, 2, block, rows)
                out = take(grid, 1 - core, 2), take(grid, core, 2)
            return add(out[1], swap(out[0], CORE)).astype(BF16).reshape(depth, 2, block, rows)

        def scatter(own, other, during):
            cut = block // 4 // 16 * 16
            rest = block - cut
            half = cut + rest // 2

            def planes(own, other, half):
                both, by_role = take(other, 1 - pair, 0), take(other, pair, 0)
                by_pair, kept = take(own, 1 - pair, 0), take(own, pair, 0)
                axis = both.ndim - 2
                low = lambda array: lax.slice_in_dim(array, 0, half, axis=axis)
                high = lambda array: lax.slice_in_dim(array, half, array.shape[axis], axis=axis)
                from_pair = swap(low(both), PAIR)
                from_role = swap(high(both), ROLE)
                by_role = jnp.concatenate([add(low(by_role), from_pair).astype(BF16), high(by_role)], axis=axis)
                by_pair = jnp.concatenate([low(by_pair), add(high(by_pair), from_role).astype(BF16)], axis=axis)
                return add(kept, swap(by_role, ROLE), swap(by_pair, PAIR)).astype(BF16)

            result = []
            if cut:
                images = jnp.stack([own[:, :, :cut], other[:, :, :cut]], axis=1)
                images = outer_sum(images).astype(BF16)
            kept = planes(own[:, :, cut:].swapaxes(0, 1), other[:, :, cut:].swapaxes(0, 1), rest // 32 * 16 or rest // 2)
            if cut:
                kept, images = lax.optimization_barrier((kept, images))
                result.append(
                    add(
                        take(images[0], pair, 0),
                        swap(take(images[0], 1 - pair, 0), PAIR),
                        swap(take(images[1], pair, 0), ROLE),
                        swap(take(images[1], 1 - pair, 0), ROLE | PAIR),
                    )
                )
            result.append(outer_sum(kept))
            return jnp.concatenate(result, axis=0), during()

        share = rows // 2
        near = swap(lax.dynamic_slice_in_dim(latents, core * share, share, 0), ROLE)

        preact, hidden, scale, *out = student(place, (latents,), student_up, student_down, shards)
        made = student_sum(core_sum(out)).astype(BF16)
        noise = fresh_noise.T.astype(F32)
        blended = ((1.0 - own_level) * made.astype(F32) + own_level * noise).astype(BF16)
        slope = gelu_slope(preact) * scale
        blended, near, slope = lax.optimization_barrier((blended, near, slope))
        far = swap(near, CORE)

        def scored(pieces, layout, level):
            return score(place, (polarity * level)[None], pieces, layout, score_up[0], score_down[0], shards)

        _, (pieces, layout), out = gather(blended, lambda *own: scored(*own, own_level))
        tokens_other, out = lax.optimization_barrier(((near, far), out))
        own_sum = core_sum(out)
        other_sum = core_sum(scored(pieces, layout, other_level))

        def other_forward():
            slope_other, hidden_other, _ = student(place, tokens_other, student_up, None, shards)
            return hidden_other, slope_other

        update, (hidden_other, slope_other) = scatter(own_sum, other_sum, other_forward)
        update, hidden_other, slope_other = lax.optimization_barrier((update.astype(BF16), hidden_other, slope_other))
        (pieces, layout), (pieces_other, layout_other), inward = gather(
            update, lambda *own: inward_gradient(place, *own, student_down, slope, shards)
        )
        grad_up, grad_down = weight_gradients(
            place, (pieces, pieces_other), (layout, layout_other), student_down, slope_other,
            (hidden, hidden_other), ((latents,), tokens_other), inward, shards,
        )
        return (made.T, grad_up, grad_down)

    return body


def solution(mesh):
    return jax.shard_map(
        make_body(mesh.shape["role"], mesh.shape["tp"]),
        mesh=mesh,
        in_specs=(
            P("role", None),
            P("role", "tp"),
            P(),
            P(None, "tp"),
            P("tp", None),
            P("role", None, "tp"),
            P("role", "tp", None),
        ),
        out_specs=(P("role", "tp"), P(None, "tp"), P("tp", None)),
        check_vma=False,
    )
```
